256 devices in a mesh: tm: 16 (over z, y_lo), mesh: 16 (over y_hi, x, core).
Axes of the slice: x: 4, y: 4 (y_hi: 2, y_lo: 2; y = y_hi * 2 + y_lo), z: 8, core: 2. Of those that a mesh axis runs over, the one named last changes fastest.
Arguments:
- adjoint: bfloat16 [2, 16, 128, 320, 128], P(None, 'tm', 'mesh'), may hold values from -6 to 6
- source: bfloat16 [2, 16, 128, 320, 128], P(None, 'tm', 'mesh'), may hold values from -6 to 6
- block_inverse: bfloat16 [2, 16, 128, 320, 320], P(None, 'tm', 'mesh'), may hold values from -1 to 1
- face_partials: bfloat16 [2, 16, 128, 6, 80, 320], P(None, 'tm', 'mesh'), may hold values from -0.625 to 0.625
- mass: float32 [128, 320], P('mesh'), may hold values from 0.4 to 2.5
Outputs:
- updated: bfloat16 [2, 16, 128, 320, 128], P(None, 'tm', 'mesh')
The draws below stay inside these ranges and needn't reach their ends.
All inputs are finite; a program needn't handle non-finite values.
Results may differ from the reference program's by a relative error of at most 0.017.
Values may be sent and summed in bfloat16 or wider, within the bound.
No kernel may reach another device: no remote copies, remote signals or barrier semaphores. Data moves between devices by JAX's collectives and lax.ppermute only.
A program may use at most 128 MiB of HBM per device.

```python
import math
import jax
import jax.numpy as jnp
from jax import lax

VARS = 5
P1 = 4
EY = 4
EZ = 2
RHS = 128
BLOCK = 320
FACE = 80
LAYERS = 16
ELEMS = 128
INST_HALF = 16
TIMES = 32


def draw_block_inverse(key, part):
    key = jax.random.fold_in(key, 7)
    shape = (2, INST_HALF, ELEMS, BLOCK, BLOCK)
    noise = jnp.clip(jax.random.normal(key, shape, jnp.float32), -4.0, 4.0)
    identity = jnp.eye(BLOCK, dtype=jnp.float32)
    return (0.3 * identity + 0.3 / math.sqrt(BLOCK) * noise).astype(jnp.bfloat16)


def block_scale(key, dims, cuts, low, high):
    factor_of = 1.0
    for position, shards_of in cuts:
        draws = jax.random.uniform(jax.random.fold_in(jax.random.fold_in(key, 6), position), (shards_of,), jnp.float32, low / len(cuts), high / len(cuts))
        factor_of = factor_of * jnp.repeat(jnp.exp(draws), dims[position] // shards_of).reshape((-1,) + (1,) * (len(dims) - 1 - position))
    return factor_of


def normal_values(stream_key, dims, deviation, most, split=(), kind=jnp.bfloat16):
    factor_of = block_scale(stream_key, dims, split, -0.22, 0.18) if split else 1.0
    result = jax.random.normal(stream_key, dims, jnp.float32) * deviation * factor_of
    return jnp.minimum(jnp.maximum(result, -most), most).astype(kind)


def setup_inputs(seed: int = 0) -> dict:
    keys = jax.random.split(jax.random.key(seed), 6)
    return {
        "adjoint": normal_values(keys[0], (2, INST_HALF, ELEMS, BLOCK, RHS), 1.0, 6.0, ((1, 16), (2, 16))),
        "source": normal_values(keys[1], (2, INST_HALF, ELEMS, BLOCK, RHS), 1.0, 6.0, ((1, 16), (2, 16))),
        "block_inverse": draw_block_inverse(jax.random.fold_in(keys[5], 71), 0),
        "face_partials": normal_values(keys[3], (2, INST_HALF, ELEMS, 6, FACE, BLOCK), FACE ** -0.5, 0.625, ((1, 16), (2, 16))),
        "mass": jnp.clip(jnp.exp(math.log(2.5) - 1.8325814 * jax.random.uniform(keys[4], (ELEMS, BLOCK), jnp.float32) ** block_scale(keys[4], (ELEMS, BLOCK), ((0, 16),), -0.2, 0.2)), 0.4, 2.5),
    }


OMEGA_TIME = 0.25


def time_weights(source_index, target_index, period):
    offset = source_index - target_index
    parity = jnp.mod(offset, 2)
    signs = (1 - 2 * parity).astype(jnp.float32)
    angle = (math.pi / period) * offset.astype(jnp.float32)
    is_self = offset == 0
    sine = jnp.where(is_self, jnp.ones_like(angle), jnp.sin(angle))
    return jnp.where(is_self, jnp.zeros_like(angle), 0.5 * signs * jnp.cos(angle) / sine)


def neighbour_traces(field, lower_rim, upper_rim):
    x_low = field[:, :, :, :, :, -1]
    x_high = field[:, :, :, :, :, 0]
    minus_x = jnp.concatenate([lower_rim[:, None], x_low[:, :-1]], axis=1)
    plus_x = jnp.concatenate([x_high[:, 1:], upper_rim[:, None]], axis=1)
    minus_y = jnp.roll(field[:, :, :, :, :, :, -1], 1, axis=2)
    plus_y = jnp.roll(field[:, :, :, :, :, :, 0], -1, axis=2)
    z_low = field[:, :, :, :, :, :, :, -1]
    z_high = field[:, :, :, :, :, :, :, 0]
    blank = jnp.zeros_like(z_low[:, :, :, :1])
    minus_z = jnp.concatenate([blank, z_low[:, :, :, :-1]], axis=3)
    plus_z = jnp.concatenate([z_high[:, :, :, 1:], blank], axis=3)
    return jnp.stack([minus_x, plus_x, minus_y, plus_y, minus_z, plus_z], axis=4)


def reference(adjoint, source, block_inverse, face_partials, mass):
    highest = lax.Precision.HIGHEST
    flat = adjoint.reshape(TIMES, ELEMS, BLOCK, RHS)
    instance = jnp.arange(TIMES, dtype=jnp.int32)
    weights = time_weights(instance[:, None], instance[None, :], TIMES)
    by_element = jnp.swapaxes(flat, 0, 1)

    def mix_element(column):
        return jnp.einsum('st,sqr->tqr', weights, column.astype(jnp.float32),
                          precision=highest).astype(jnp.bfloat16)

    spectral = jnp.swapaxes(lax.map(mix_element, by_element), 0, 1)

    def update_instance(operands):
        field, forcing, inverse, partials, mixed = operands
        grid = field.reshape(1, LAYERS, EY, EZ, VARS, P1, P1, P1, RHS)
        rim_zero = jnp.zeros((1, EY, EZ, VARS, P1, P1, RHS), field.dtype)
        traces = neighbour_traces(grid, rim_zero, rim_zero).reshape(ELEMS, 6, FACE, RHS)
        coupling = jnp.einsum('efkq,efkr->eqr', partials.astype(jnp.float32),
                              traces.astype(jnp.float32), precision=highest)
        residual = (forcing.astype(jnp.float32) - coupling
                    - OMEGA_TIME * mass[:, :, None] * mixed.astype(jnp.float32)).astype(jnp.bfloat16)
        return jnp.einsum('eqp,epr->eqr', inverse.astype(jnp.float32), residual.astype(jnp.float32),
                          precision=highest).astype(jnp.bfloat16)

    updated = lax.map(update_instance, (
        flat,
        source.reshape(TIMES, ELEMS, BLOCK, RHS),
        block_inverse.reshape(TIMES, ELEMS, BLOCK, BLOCK),
        face_partials.reshape(TIMES, ELEMS, 6, FACE, BLOCK),
        spectral))
    return updated.reshape(2, INST_HALF, ELEMS, BLOCK, RHS)
```

```python
import math

import jax
import jax.numpy as jnp
import numpy as np
from jax import lax
from jax.experimental import pallas as pl
from jax.experimental.pallas import tpu as pltpu
from jax.sharding import PartitionSpec as P

VARS = 5
P1 = 4
EY = 4
EZ = 2
LAY_DEV = 1
RHS = 128
BLOCK = 320
FACE = 80
OMEGA_TIME = 0.25

RING = 8
TIMES = 32
HALF = 16
ROLES = 4
ORDER = (1, 0, 3, 2)
OWN, OTHER = 0, 1
FAR = 3
AHEAD = 2
PIECE = (2, BLOCK, RHS)


def spectral_weight(offset):
    offset = offset % TIMES
    if offset in (0, HALF):
        return 0.0
    return 0.5 * (-1) ** offset / math.tan(math.pi * offset / TIMES)


def weight_slot(source_step, target_step, source_column, target_column):
    row = (target_step + AHEAD) * (2 * FAR + 1) + source_step + FAR
    return 2 * (4 * row + 2 * source_column + target_column)


def weight_table():
    table = np.zeros((HALF, 8 * (2 * AHEAD + 1) * (2 * FAR + 1)), np.float32)
    for member in range(HALF):
        z, y = divmod(member, 2)
        for target_step in range(-AHEAD, AHEAD + 1):
            for source_step in range(-FAR, FAR + 1):
                for source_column in (OWN, OTHER):
                    for target_column in (OWN, OTHER):
                        source = (z + source_step) % RING * 2 + (y ^ source_column)
                        target = (z + target_step) % RING * 2 + (y ^ target_column)
                        near = spectral_weight(source - target)
                        far = spectral_weight(source - target + HALF)
                        slot = weight_slot(source_step, target_step, source_column, target_column)
                        table[member, slot] = 0.5 * (near + far)
                        table[member, slot + 1] = 0.5 * (near - far)
    return table


def element_table():
    table = np.zeros((HALF, 2 * ROLES), np.int32)
    for member in range(HALF):
        z, y = divmod(member, 2)
        for place, role in enumerate(ORDER):
            table[member, place] = y * ROLES + (z - role) % ROLES
            table[member, ROLES + place] = (1 - y) * ROLES + (z - role) % ROLES
    return table


def column_pairs(step, swap):
    return [
        (z * 2 + y, (z + step) % RING * 2 + (y ^ swap)) for z in range(RING) for y in range(2)
    ]


def send(value, step, swap=0):
    return lax.ppermute(value, "tm", column_pairs(step, swap))


def combine(weights, groups, dtypes, rows=80):
    operands, operand_of = [], {}
    for sources, _ in groups:
        for array, place, _, _ in sources:
            if (id(array), place) not in operand_of:
                operand_of[id(array), place] = len(operands)
                operands.append((array, place))
    slots = [0] * len(dtypes)
    stores = []
    for _, targets in groups:
        placed = []
        for step, column, output in targets:
            placed.append((step, column, output, slots[output]))
            slots[output] += 1
        stores.append(placed)

    def kernel(weights_ref, *refs):
        inputs, outputs = refs[: len(operands)], refs[len(operands):]
        for (sources, _), targets in zip(groups, stores):
            sums = [None] * len(targets)
            for array, place, source_step, source_column in sources:
                ref = inputs[operand_of[id(array), place]]
                first = ref[0, 0].astype(jnp.float32)
                second = ref[0, 1].astype(jnp.float32)
                plus, minus = first + second, first - second
                for index, (step, column, _, _) in enumerate(targets):
                    if source_step == step and source_column == column:
                        continue
                    slot = weight_slot(source_step, step, source_column, column)
                    term = (weights_ref[slot] * plus, weights_ref[slot + 1] * minus)
                    if sums[index] is None:
                        sums[index] = term
                    else:
                        sums[index] = (sums[index][0] + term[0], sums[index][1] + term[1])
            for (plus, minus), (_, _, output, slot) in zip(sums, targets):
                outputs[output][slot, 0] = (plus + minus).astype(outputs[output].dtype)
                outputs[output][slot, 1] = (plus - minus).astype(outputs[output].dtype)

    pairs = sum(len(sources) * len(targets) for sources, targets in groups)
    moved = 2 * BLOCK * RHS * (2 * len(operands) + 2 * sum(slots))
    return pl.pallas_call(
        kernel,
        grid=(BLOCK // rows,),
        in_specs=[pl.BlockSpec(memory_space=pltpu.SMEM)]
        + [
            pl.BlockSpec((1, 2, rows, RHS), lambda i, place=place: (place, 0, i, 0))
            for _, place in operands
        ],
        out_specs=[pl.BlockSpec((count, 2, rows, RHS), lambda i: (0, 0, i, 0)) for count in slots],
        out_shape=[
            jax.ShapeDtypeStruct((count, *PIECE), dtype) for count, dtype in zip(slots, dtypes)
        ],
        cost_estimate=pl.CostEstimate(
            flops=4 * pairs * BLOCK * RHS, bytes_accessed=moved, transcendentals=0
        ),
    )(weights, *[array for array, _ in operands])


def finish(elements, base, scaled_mass, block_inverse, own, passed, near, across):
    def kernel(elements_ref, base_ref, mass_ref, inverse_ref, own_ref, passed_ref, *refs):
        near_refs, across_refs = refs[:ROLES], refs[ROLES: 2 * ROLES]
        out_ref, spectral = refs[2 * ROLES:]
        step = pl.program_id(0)
        for place in range(ROLES):
            @pl.when(step == place)
            def _():
                spectral[...] = own_ref[0] + near_refs[place][0].astype(jnp.float32)

            @pl.when(step == ROLES + place)
            def _():
                spectral[...] = passed_ref[0].astype(jnp.float32) + across_refs[place][0].astype(jnp.float32)

        for half in range(2):
            mixed = spectral[half].astype(jnp.bfloat16).astype(jnp.float32)
            residual = (base_ref[half, 0] - mass_ref[0] * mixed).astype(jnp.bfloat16)
            out_ref[half, 0] = jnp.dot(
                inverse_ref[half, 0], residual, preferred_element_type=jnp.float32
            ).astype(jnp.bfloat16)

    whole = pl.BlockSpec((1, *PIECE), lambda i, e: (0, 0, 0, 0))
    return pl.pallas_call(
        kernel,
        grid_spec=pltpu.PrefetchScalarGridSpec(
            num_scalar_prefetch=1,
            grid=(2 * ROLES,),
            in_specs=[
                pl.BlockSpec((2, 1, BLOCK, RHS), lambda i, e: (0, e[i], 0, 0)),
                pl.BlockSpec((1, BLOCK, RHS), lambda i, e: (e[i], 0, 0)),
                pl.BlockSpec((2, 1, BLOCK, BLOCK), lambda i, e: (0, e[i], 0, 0)),
                pl.BlockSpec((1, *PIECE), lambda i, e: (jnp.minimum(i, ROLES - 1), 0, 0, 0)),
                pl.BlockSpec((1, *PIECE), lambda i, e: (jnp.maximum(i - ROLES, 0), 0, 0, 0)),
            ]
            + [whole] * (2 * ROLES),
            out_specs=pl.BlockSpec((2, 1, BLOCK, RHS), lambda i, e: (0, e[i], 0, 0)),
            scratch_shapes=[pltpu.VMEM(PIECE, jnp.float32)],
        ),
        out_shape=jax.ShapeDtypeStruct((2, 2 * ROLES, BLOCK, RHS), jnp.bfloat16),
        cost_estimate=pl.CostEstimate(
            flops=4 * 2 * ROLES * BLOCK * BLOCK * RHS, bytes_accessed=10_000_000, transcendentals=0
        ),
    )(elements, base, scaled_mass, block_inverse, own, passed, *near, *across)


def from_behind(value, axis, steps):
    count = lax.axis_size(axis)
    first, last = (max(0, -steps), min(count, count - steps))
    return lax.ppermute(value, axis, [(source, source + steps) for source in range(first, last)])


def neighbour_traces(field, lower_rim, upper_rim):
    x_low = field[:, :, :, :, :, -1]
    x_high = field[:, :, :, :, :, 0]
    minus_x = jnp.concatenate([lower_rim[:, None], x_low[:, :-1]], axis=1)
    plus_x = jnp.concatenate([x_high[:, 1:], upper_rim[:, None]], axis=1)
    minus_y = jnp.roll(field[:, :, :, :, :, :, -1], 1, axis=2)
    plus_y = jnp.roll(field[:, :, :, :, :, :, 0], -1, axis=2)
    z_low = field[:, :, :, :, :, :, :, -1]
    z_high = field[:, :, :, :, :, :, :, 0]
    blank = jnp.zeros_like(z_low[:, :, :, :1])
    minus_z = jnp.concatenate([blank, z_low[:, :, :, :-1]], axis=3)
    plus_z = jnp.concatenate([z_high[:, :, :, 1:], blank], axis=3)
    return jnp.stack([minus_x, plus_x, minus_y, plus_y, minus_z, plus_z], axis=4)


def per_device(adjoint, source, block_inverse, face_partials, mass):
    member = lax.axis_index("tm")
    field = adjoint[:, 0]
    weights = lax.dynamic_index_in_dim(jnp.asarray(weight_table()), member, 0, keepdims=False)
    elements = lax.dynamic_index_in_dim(jnp.asarray(element_table()), member, 0, keepdims=False)

    def picked(first, last):
        return jnp.stack([
            lax.dynamic_index_in_dim(field, elements[place], 1, keepdims=False)
            for place in range(first, last)
        ])

    mine = picked(0, ROLES)
    other = send(picked(ROLES, 2 * ROLES), 0, 1)
    up, down = [], []
    for held in (mine, other):
        up1 = send(held[1:4], 1)
        down1 = send(held[0:3], -1)
        up2 = send(up1[1:3], 1)
        down2 = send(down1[0:2], -1)
        up3 = send(up2[1:2], 1)
        down3 = send(down2[0:1], -1)
        up.append((held, up1, up2, up3))
        down.append((held, down1, down2, down3))

    def sources(entries):
        return [
            (stream[column][level], place, step, column)
            for column in (OWN, OTHER)
            for stream, level, place, step in entries
        ]

    role_one = sources([(up, 0, 0, 0), (up, 1, 0, -1), (up, 2, 0, -2), (up, 3, 0, -3)])
    role_two = sources([(down, 0, 3, 0), (down, 1, 2, 1), (down, 2, 1, 2), (down, 3, 0, 3)])
    role_zero = sources([(up, 0, 1, 0), (up, 1, 1, -1), (up, 2, 1, -2), (down, 1, 0, 1)])
    role_three = sources([(up, 0, 2, 0), (down, 1, 1, 1), (down, 2, 0, 2), (up, 1, 2, -1)])
    bf16 = jnp.bfloat16
    f32 = jnp.float32
    here = [(0, OWN, 0), (0, OTHER, 1)]

    def ahead(sign):
        return [(2 * sign, OWN, 0), (2 * sign, OTHER, 1), (sign, OWN, 2), (sign, OTHER, 3)]

    outer_own, outer_other = combine(weights, [(role_zero, here), (role_three, here)], [f32, bf16])
    passed_outer = send(outer_other, 0, 1)
    up_sums = combine(weights, [(role_one, ahead(1))], [bf16] * 4)
    down_sums = combine(weights, [(role_two, ahead(-1))], [bf16] * 4)
    up_far, up_far_across = send(up_sums[0], 2), send(up_sums[1], 2, 1)
    down_far, down_far_across = send(down_sums[0], -2), send(down_sums[1], -2, 1)
    up_near, up_near_across = send(up_sums[2], 1), send(up_sums[3], 1, 1)
    down_near, down_near_across = send(down_sums[2], -1), send(down_sums[3], -1, 1)
    inner_own, inner_other = combine(weights, [(role_one, here), (role_two, here)], [f32, bf16])
    passed_inner = send(inner_other, 0, 1)

    elements_here = adjoint.shape[2]
    grid = field.reshape(2, LAY_DEV, EY, EZ, VARS, P1, P1, P1, RHS)
    lower_rim = from_behind(grid[:, -1, :, :, :, -1], "mesh", 1)
    upper_rim = from_behind(grid[:, 0, :, :, :, 0], "mesh", -1)
    traces = neighbour_traces(grid, lower_rim, upper_rim).reshape(2, elements_here, 6, FACE, RHS)
    coupling = jnp.einsum(
        "hefkq,hefkr->heqr", face_partials[:, 0], traces, preferred_element_type=jnp.float32
    )
    base = source[:, 0].astype(jnp.float32) - coupling
    scaled_mass = jnp.broadcast_to((OMEGA_TIME * mass)[:, :, None], (elements_here, BLOCK, RHS))

    def in_order(outer, inner):
        return jnp.concatenate([inner[0:1], outer, inner[1:2]])

    updated = finish(
        elements, base, scaled_mass, block_inverse[:, 0],
        in_order(outer_own, inner_own), in_order(passed_outer, passed_inner),
        [down_near, down_far, up_far, up_near],
        [down_near_across, down_far_across, up_far_across, up_near_across],
    )
    return updated[:, None]


def solution(mesh):
    return jax.shard_map(
        per_device,
        mesh=mesh,
        in_specs=(
            P(None, "tm", "mesh", None, None),
            P(None, "tm", "mesh", None, None),
            P(None, "tm", "mesh", None, None),
            P(None, "tm", "mesh", None, None, None),
            P("mesh", None),
        ),
        out_specs=P(None, "tm", "mesh", None, None),
        check_vma=False,
    )
```

```python
import math

import jax
import jax.numpy as jnp
import numpy as np
from jax import lax
from jax.experimental import pallas as pl
from jax.experimental.pallas import tpu as pltpu
from jax.sharding import PartitionSpec as P

VARS = 5
P1 = 4
EY = 4
EZ = 2
RHS = 128
BLOCK = 320
FACE = 80
OMEGA_TIME = 0.25

RING = 8
TIMES = 32
HALF = 16
ROLES = 4
ORDER = (1, 0, 3, 2)
OWN, OTHER = 0, 1
FAR = 3
AHEAD = 2
PIECE = (2, BLOCK, RHS)
VMEM = 8 << 20
BRIEF = pl.CostEstimate(flops=1, bytes_accessed=1, transcendentals=0)


def spectral_weight(offset):
    offset = offset % TIMES
    if offset in (0, HALF):
        return 0.0
    return 0.5 * (-1) ** offset / math.tan(math.pi * offset / TIMES)


def weight_slot(source_step, target_step, source_column, target_column):
    row = (target_step + AHEAD) * (2 * FAR + 1) + source_step + FAR
    return 2 * (4 * row + 2 * source_column + target_column)


def weight_table():
    table = np.zeros((HALF, 8 * RHS), np.float32)
    for member in range(HALF):
        z, y = divmod(member, 2)
        for target_step in range(-AHEAD, AHEAD + 1):
            for source_step in range(-FAR, FAR + 1):
                for source_column in (OWN, OTHER):
                    for target_column in (OWN, OTHER):
                        source = (z + source_step) % RING * 2 + (y ^ source_column)
                        target = (z + target_step) % RING * 2 + (y ^ target_column)
                        near = spectral_weight(source - target)
                        far = spectral_weight(source - target + HALF)
                        slot = weight_slot(source_step, target_step, source_column, target_column)
                        table[member, slot] = 0.5 * (near + far)
                        table[member, slot + 1] = 0.5 * (near - far)
    return table.reshape(HALF, 8, RHS)


def element_at(member, place, column):
    z, y = member // 2, member % 2
    half = y if column == OWN else 1 - y
    return half * ROLES + (z + ROLES - (place ^ 1)) % ROLES


def column_pairs(step, swap):
    return [
        (z * 2 + y, (z + step) % RING * 2 + (y ^ swap)) for z in range(RING) for y in range(2)
    ]


def send(value, step, swap=0):
    return lax.ppermute(value, "tm", column_pairs(step, swap))


def move(plan, operands, shapes, tokens=(), dtype=jnp.bfloat16):
    def kernel(*refs):
        refs = refs[len(tokens):]
        copies = [
            pltpu.make_async_copy(origin, target, refs[-1].at[index])
            for index, (origin, target) in enumerate(plan(*refs[:-1]))
        ]
        for copy in copies:
            copy.start()
        for copy in copies:
            copy.wait()

    return pl.pallas_call(
        kernel,
        in_specs=[pl.BlockSpec(memory_space=pl.ANY)] * len(tokens)
        + [pl.BlockSpec(memory_space=pl.ANY)] * len(operands),
        out_specs=[pl.BlockSpec(memory_space=pl.ANY)] * len(shapes),
        out_shape=[jax.ShapeDtypeStruct(shape, dtype) for shape in shapes],
        scratch_shapes=[pltpu.SemaphoreType.DMA((32,))],
        compiler_params=pltpu.CompilerParams(vmem_limit_bytes=VMEM),
        cost_estimate=BRIEF,
    )(*tokens, *operands)


def pick(field, tokens):
    def plan(field_ref, mine_ref, up_ref, down_ref, theirs_ref):
        member = lax.axis_index("tm")
        moves = []
        for place in range(ROLES):
            own = field_ref.at[:, element_at(member, place, OWN)]
            moves.append((field_ref.at[:, element_at(member, place, OTHER)], theirs_ref.at[place]))
            if place > 0:
                moves.append((own, up_ref.at[place - 1]))
            if place < ROLES - 1:
                moves.append((own, down_ref.at[place]))
            moves.append((own, mine_ref.at[place]))
        return moves

    return move(plan, [field], [(count, *PIECE) for count in (ROLES, ROLES - 1, ROLES - 1, ROLES)], tokens)


def rims(field, token):
    edge = P1 * P1

    def plan(field_ref, last_ref, first_ref):
        moves = []
        for variable in range(VARS):
            target = pl.ds(variable * edge, edge)
            for ref, node in ((last_ref, P1 - 1), (first_ref, 0)):
                origin = pl.ds((variable * P1 + node) * edge, edge)
                moves.append((field_ref.at[:, :, origin], ref.at[:, :, target]))
        return moves

    return move(plan, [field], [(2, field.shape[1], FACE, RHS)] * 2, [token])


def messages(parts, tokens=()):
    def plan(*refs):
        return [
            (ref.at[first:last], target)
            for ref, target, (_, first, last) in zip(refs, refs[len(parts):], parts)
        ]

    shapes = [(last - first, *PIECE) for _, first, last in parts]
    return move(plan, [held for held, _, _ in parts], shapes, tokens)


def combine(weights, groups, dtypes, tokens=(), rows=16):
    operands, operand_of = [], {}
    for sources, _ in groups:
        for array, _, _, _ in sources:
            if id(array) not in operand_of:
                operand_of[id(array)] = len(operands)
                operands.append(array)
    slots = [0] * len(dtypes)
    stores = []
    for _, targets in groups:
        placed = []
        for step, column, output in targets:
            placed.append((step, column, output, slots[output]))
            slots[output] += 1
        stores.append(placed)

    def kernel(weights_ref, *refs):
        refs = refs[len(tokens):]
        inputs, outputs = refs[: len(operands)], refs[len(operands):]
        for (sources, _), targets in zip(groups, stores):
            @pl.loop(0, BLOCK // rows)
            def _(chunk):
                span = pl.ds(pl.multiple_of(chunk * rows, rows), rows)
                sums = [None] * len(targets)
                for array, place, source_step, source_column in sources:
                    ref = inputs[operand_of[id(array)]]
                    first = ref[place, 0, span].astype(jnp.float32)
                    second = ref[place, 1, span].astype(jnp.float32)
                    plus, minus = first + second, first - second
                    for index, (step, column, _, _) in enumerate(targets):
                        if source_step == step and source_column == column:
                            continue
                        slot = weight_slot(source_step, step, source_column, column)
                        row, lane = divmod(slot, RHS)
                        term = (weights_ref[row, lane] * plus, weights_ref[row, lane + 1] * minus)
                        if sums[index] is None:
                            sums[index] = term
                        else:
                            sums[index] = (sums[index][0] + term[0], sums[index][1] + term[1])
                for (plus, minus), (_, _, output, slot) in zip(sums, targets):
                    outputs[output][slot, 0, span] = (plus + minus).astype(outputs[output].dtype)
                    outputs[output][slot, 1, span] = (plus - minus).astype(outputs[output].dtype)

    vmem = pl.BlockSpec(memory_space=pltpu.VMEM)
    return pl.pallas_call(
        kernel,
        in_specs=[pl.BlockSpec(memory_space=pltpu.SMEM)]
        + [pl.BlockSpec(memory_space=pl.ANY)] * len(tokens)
        + [vmem] * len(operands),
        out_specs=[vmem] * len(slots),
        out_shape=[
            jax.ShapeDtypeStruct((count, *PIECE), dtype) for count, dtype in zip(slots, dtypes)
        ],
        compiler_params=pltpu.CompilerParams(vmem_limit_bytes=VMEM),
        cost_estimate=BRIEF,
    )(weights, *tokens, *operands)


def settle(outer, inner, first, second, tokens):
    def kernel(*refs):
        outer_ref, inner_ref, first_ref, second_ref, out_ref = refs[len(tokens):]
        for position, ref in enumerate((first_ref, second_ref)):
            total = inner_ref[position] + ref[1].astype(jnp.float32)
            out_ref[position] = total.astype(jnp.bfloat16)
            out_ref[2 + position] = outer_ref[position]

    vmem = pl.BlockSpec(memory_space=pltpu.VMEM)
    return pl.pallas_call(
        kernel,
        in_specs=[pl.BlockSpec(memory_space=pl.ANY)] * len(tokens) + [vmem] * 4,
        out_specs=vmem,
        out_shape=jax.ShapeDtypeStruct((ROLES, *PIECE), jnp.bfloat16),
        compiler_params=pltpu.CompilerParams(vmem_limit_bytes=VMEM),
        cost_estimate=BRIEF,
    )(*tokens, outer, inner, first, second)


def finish(member, base, scale, block_inverse, places, terms, before=None):
    count = len(places)

    def element(step, member_ref):
        index = element_at(member_ref[0], *places[0])
        for position in range(1, count):
            index = jnp.where(step == position, element_at(member_ref[0], *places[position]), index)
        return index

    arrays = []
    for array, _ in sum(terms, []):
        if not any(array is known for known in arrays):
            arrays.append(array)

    def find(refs, entry):
        for ref, array in zip(refs, arrays):
            if array is entry[0]:
                return ref[entry[1]].astype(jnp.float32)

    def kernel(member_ref, base_ref, scale_ref, inverse_ref, *refs):
        out_ref, spectral = refs[-2:]
        step = pl.program_id(0)
        for position in range(count):
            @pl.when(step == position)
            def _():
                total = sum(find(refs, term) for term in terms[position])
                spectral[...] = total.astype(jnp.bfloat16)

        for half in range(2):
            mixed = spectral[half].astype(jnp.float32)
            residual = (base_ref[half, 0] - scale_ref[0] * mixed).astype(jnp.bfloat16)
            out_ref[half, 0] = jnp.dot(
                inverse_ref[half, 0], residual, preferred_element_type=jnp.float32
            ).astype(jnp.bfloat16)

    whole = pl.BlockSpec(memory_space=pltpu.VMEM)
    by_element = pl.BlockSpec((2, 1, BLOCK, RHS), lambda i, m: (0, element(i, m), 0, 0))
    operands = [base, scale, block_inverse, *arrays]
    specs = [
        by_element,
        pl.BlockSpec((1, BLOCK, RHS), lambda i, m: (element(i, m), 0, 0)),
        pl.BlockSpec((2, 1, BLOCK, BLOCK), lambda i, m: (0, element(i, m), 0, 0)),
    ] + [whole] * len(arrays)
    aliases = {}
    if before is not None:
        operands.append(before)
        specs.append(pl.BlockSpec(memory_space=pl.ANY))
        aliases = {len(operands): 0}
    return pl.pallas_call(
        kernel,
        grid_spec=pltpu.PrefetchScalarGridSpec(
            num_scalar_prefetch=1,
            grid=(count,),
            in_specs=specs,
            out_specs=by_element,
            scratch_shapes=[pltpu.VMEM(PIECE, jnp.bfloat16)],
        ),
        out_shape=jax.ShapeDtypeStruct((2, 2 * ROLES, BLOCK, RHS), jnp.bfloat16),
        input_output_aliases=aliases,
        compiler_params=pltpu.CompilerParams(vmem_limit_bytes=VMEM),
        cost_estimate=BRIEF,
    )(member, *operands)


def from_behind(value, axis, steps):
    count = lax.axis_size(axis)
    first, last = (max(0, -steps), min(count, count - steps))
    return lax.ppermute(value, axis, [(source, source + steps) for source in range(first, last)])


def trace_rows():
    rows = np.zeros((4, FACE, BLOCK), np.float32)
    for outer in range(VARS * P1):
        for inner in range(P1):
            rows[0, outer * P1 + inner, (outer * P1 + P1 - 1) * P1 + inner] = 1
            rows[1, outer * P1 + inner, outer * P1 * P1 + inner] = 1
            rows[2, outer * P1 + inner, (outer * P1 + inner) * P1 + P1 - 1] = 1
            rows[3, outer * P1 + inner, (outer * P1 + inner) * P1] = 1
    return rows.reshape(4 * FACE, BLOCK)


def transposed_dot(left, right):
    return lax.dot_general(left, right, (((0,), (0,)), ((), ())), preferred_element_type=jnp.float32)


def couple(field, lower, upper, source, face_partials, mass, tokens):
    elements = field.shape[1]

    def kernel(*refs):
        (rows_ref, field_ref, lower_ref, upper_ref, source_ref, partials_ref, mass_ref,
         out_ref, scale_ref, token_ref, picked) = refs[len(tokens):]
        element = pl.program_id(0)

        @pl.when(element == 0)
        def _():
            @pl.loop(0, elements)
            def _(index):
                for half in range(2):
                    picked[half, index] = jnp.dot(
                        rows_ref[...], field_ref[half, index], preferred_element_type=jnp.float32
                    ).astype(jnp.bfloat16)

        token_ref[...] = jnp.zeros_like(token_ref)
        row = OMEGA_TIME * mass_ref[pl.ds(element, 1), :]
        scale_ref[0] = jnp.broadcast_to(row, (RHS, BLOCK)).T
        pitch, span = element // EZ, element % EZ
        behind = (pitch + EY - 1) % EY * EZ + span
        ahead = (pitch + 1) % EY * EZ + span
        across = element + 1 - 2 * span
        for half in range(2):
            low = picked[half, across, 2 * FACE: 3 * FACE]
            high = picked[half, across, 3 * FACE: 4 * FACE]
            traces = jnp.concatenate([
                lower_ref[half, 0],
                upper_ref[half, 0],
                picked[half, behind, 0: FACE],
                picked[half, ahead, FACE: 2 * FACE],
                jnp.where(span == 1, low, jnp.zeros_like(low)),
                jnp.where(span == 0, high, jnp.zeros_like(high)),
            ])
            partials = jnp.concatenate([partials_ref[half, 0, face] for face in range(6)])
            out_ref[half, 0] = source_ref[half, 0].astype(jnp.float32) - lax.dot_general(
                partials, traces, (((0,), (0,)), ((), ())), preferred_element_type=jnp.float32
            )

    whole = pl.BlockSpec(memory_space=pltpu.VMEM)
    by_element = pl.BlockSpec((2, 1, BLOCK, RHS), lambda i: (0, i, 0, 0))
    rim = pl.BlockSpec((2, 1, FACE, RHS), lambda i: (0, i, 0, 0))
    return pl.pallas_call(
        kernel,
        grid=(elements,),
        in_specs=[pl.BlockSpec(memory_space=pl.ANY)] * len(tokens) + [
            whole, whole, rim, rim, by_element,
            pl.BlockSpec((2, 1, 6, FACE, BLOCK), lambda i: (0, i, 0, 0, 0)),
            whole,
        ],
        out_specs=[
            by_element,
            pl.BlockSpec((1, BLOCK, RHS), lambda i: (i, 0, 0)),
            pl.BlockSpec((8, RHS), lambda i: (0, 0)),
        ],
        out_shape=[
            jax.ShapeDtypeStruct(field.shape, jnp.float32),
            jax.ShapeDtypeStruct(field.shape[1:], jnp.float32),
            jax.ShapeDtypeStruct((8, RHS), jnp.float32),
        ],
        scratch_shapes=[pltpu.VMEM(field.shape, jnp.bfloat16)],
        compiler_params=pltpu.CompilerParams(vmem_limit_bytes=VMEM),
        cost_estimate=BRIEF,
    )(
        *tokens, jnp.asarray(trace_rows(), jnp.bfloat16), field, lower, upper, source,
        face_partials, mass,
    )


def per_device(adjoint, source, block_inverse, face_partials, mass):
    member = lax.axis_index("tm").reshape(1)
    field = adjoint[:, 0]
    block_inverse = block_inverse[:, 0]
    weights = move(
        lambda origin, target: [(origin.at[lax.axis_index("tm")], target)],
        [jnp.asarray(weight_table())], [(8, RHS)], dtype=jnp.float32,
    )[0]

    mine, for_up, for_down, theirs = pick(field, [member])
    other = send(theirs, 0, 1)
    up_one, down_one = [send(for_up, 1)], [send(for_down, -1)]
    last, first = rims(field, mine)
    lower_rim, upper_rim = from_behind(last, "mesh", 1), from_behind(first, "mesh", -1)
    for_up, for_down = messages([(up_one[OWN], 1, 3), (down_one[OWN], 0, 2)])
    up_two, down_two = [send(for_up, 1)], [send(for_down, -1)]
    for_up, for_down = messages(
        [(other, 1, 4), (other, 0, 3)], [for_up, lower_rim, upper_rim]
    )
    base, scale, coupled = couple(
        field, lower_rim, upper_rim, source[:, 0], face_partials[:, 0], mass, [for_up]
    )
    up_one.append(send(for_up, 1))
    down_one.append(send(for_down, -1))
    for_up, for_down = messages([(up_two[OWN], 1, 2), (down_two[OWN], 0, 1)])
    up_three, down_three = [send(for_up, 1)], [send(for_down, -1)]
    for_up, for_down = messages(
        [(up_one[OTHER], 1, 3), (down_one[OTHER], 0, 2)], [coupled]
    )
    up_two.append(send(for_up, 1))
    down_two.append(send(for_down, -1))
    for_up, for_down = messages([(up_two[OTHER], 1, 2), (down_two[OTHER], 0, 1)])
    up_three.append(send(for_up, 1))
    down_three.append(send(for_down, -1))
    up = list(zip((mine, other), up_one, up_two, up_three))
    down = list(zip((mine, other), down_one, down_two, down_three))

    def sources(entries):
        return [
            (stream[column][level], place, step, column)
            for column in (OWN, OTHER)
            for stream, level, place, step in entries
        ]

    role_one = sources([(up, 0, 0, 0), (up, 1, 0, -1), (up, 2, 0, -2), (up, 3, 0, -3)])
    role_two = sources([(down, 0, 3, 0), (down, 1, 2, 1), (down, 2, 1, 2), (down, 3, 0, 3)])
    role_zero = sources([(up, 0, 1, 0), (up, 1, 1, -1), (up, 2, 1, -2), (down, 1, 0, 1)])
    role_three = sources([(up, 0, 2, 0), (down, 1, 1, 1), (down, 2, 0, 2), (up, 1, 2, -1)])
    bf16 = jnp.bfloat16
    f32 = jnp.float32
    here = [(0, OWN, 0), (0, OTHER, 1)]

    outer_own, outer_other = combine(weights, [(role_zero, here), (role_three, here)], [f32, bf16])
    for_up, for_down, inner_own, inner_other = combine(
        weights,
        [
            (role_one, [(1, OWN, 0), (1, OTHER, 0), (0, OWN, 2), (0, OTHER, 3)]),
            (role_two, [(-1, OWN, 1), (-1, OTHER, 1), (0, OWN, 2), (0, OTHER, 3)]),
        ],
        [bf16, bf16, f32, f32],
        [outer_other],
    )
    up_near, down_near = send(for_up, 1), send(for_down, -1)
    up_far, up_far_across, down_far, down_far_across = combine(
        weights,
        [
            (role_one, [(2, OWN, 0), (2, OTHER, 1)]),
            (role_two, [(-2, OWN, 2), (-2, OTHER, 3)]),
        ],
        [bf16] * 4,
        [for_up],
    )
    token = up_far
    up_far, up_far_across = send(up_far, 2), send(up_far_across, 2, 1)
    down_far, down_far_across = send(down_far, -2), send(down_far_across, -2, 1)
    passed = send(settle(outer_other, inner_other, down_near, up_near, [token]), 0, 1)

    updated = None
    for places, terms in (
        (
            [(0, OWN), (3, OWN)],
            [[(inner_own, 0), (down_near, 0)], [(inner_own, 1), (up_near, 0)]],
        ),
        ([(0, OTHER), (3, OTHER)], [[(passed, 0)], [(passed, 1)]]),
        (
            [(1, OWN), (2, OWN), (1, OTHER), (2, OTHER)],
            [
                [(outer_own, 0), (down_far, 0)], [(outer_own, 1), (up_far, 0)],
                [(passed, 2), (down_far_across, 0)], [(passed, 3), (up_far_across, 0)],
            ],
        ),
    ):
        updated = finish(member, base, scale, block_inverse, places, terms, updated)
    return updated[:, None]


def solution(mesh):
    return jax.shard_map(
        per_device,
        mesh=mesh,
        in_specs=(
            P(None, "tm", "mesh", None, None),
            P(None, "tm", "mesh", None, None),
            P(None, "tm", "mesh", None, None),
            P(None, "tm", "mesh", None, None, None),
            P("mesh", None),
        ),
        out_specs=P(None, "tm", "mesh", None, None),
        check_vma=False,
    )
```

```python
import math

import jax
import jax.numpy as jnp
import numpy as np
from jax import lax
from jax.experimental import pallas as pl
from jax.experimental.pallas import tpu as pltpu
from jax.sharding import PartitionSpec as P

VARS = 5
P1 = 4
EY = 4
EZ = 2
RHS = 128
BLOCK = 320
FACE = 80
OMEGA_TIME = 0.25

RING = 8
TIMES = 32
HALF = 16
ROLES = 4
ORDER = (1, 0, 3, 2)
OWN, OTHER = 0, 1
FAR = 3
AHEAD = 2
PIECE = (2, BLOCK, RHS)
VMEM = 8 << 20
BRIEF = pl.CostEstimate(flops=1, bytes_accessed=1, transcendentals=0)


def spectral_weight(offset):
    offset = offset % TIMES
    if offset in (0, HALF):
        return 0.0
    return 0.5 * (-1) ** offset / math.tan(math.pi * offset / TIMES)


def weight_slot(source_step, target_step, source_column, target_column):
    row = (target_step + AHEAD) * (2 * FAR + 1) + source_step + FAR
    return 2 * (4 * row + 2 * source_column + target_column)


def weight_table():
    table = np.zeros((HALF, 8 * RHS), np.float32)
    for member in range(HALF):
        z, y = divmod(member, 2)
        for target_step in range(-AHEAD, AHEAD + 1):
            for source_step in range(-FAR, FAR + 1):
                for source_column in (OWN, OTHER):
                    for target_column in (OWN, OTHER):
                        source = (z + source_step) % RING * 2 + (y ^ source_column)
                        target = (z + target_step) % RING * 2 + (y ^ target_column)
                        near = spectral_weight(source - target)
                        far = spectral_weight(source - target + HALF)
                        slot = weight_slot(source_step, target_step, source_column, target_column)
                        table[member, slot] = 0.5 * (near + far)
                        table[member, slot + 1] = 0.5 * (near - far)
    return table.reshape(HALF, 8, RHS)


def element_at(member, place, column):
    z, y = member // 2, member % 2
    half = y if column == OWN else 1 - y
    return half * ROLES + (z + ROLES - (place ^ 1)) % ROLES


def column_pairs(step, swap):
    return [
        (z * 2 + y, (z + step) % RING * 2 + (y ^ swap)) for z in range(RING) for y in range(2)
    ]


def send(value, step, swap=0):
    return lax.ppermute(value, "tm", column_pairs(step, swap))


def move(plan, operands, shapes, tokens=(), dtype=jnp.bfloat16):
    def kernel(*refs):
        refs = refs[len(tokens):]
        copies = [
            pltpu.make_async_copy(origin, target, refs[-1].at[index])
            for index, (origin, target) in enumerate(plan(*refs[:-1]))
        ]
        for copy in copies:
            copy.start()
        for copy in copies:
            copy.wait()

    return pl.pallas_call(
        kernel,
        in_specs=[pl.BlockSpec(memory_space=pl.ANY)] * len(tokens)
        + [pl.BlockSpec(memory_space=pl.ANY)] * len(operands),
        out_specs=[pl.BlockSpec(memory_space=pl.ANY)] * len(shapes),
        out_shape=[jax.ShapeDtypeStruct(shape, dtype) for shape in shapes],
        scratch_shapes=[pltpu.SemaphoreType.DMA((32,))],
        compiler_params=pltpu.CompilerParams(vmem_limit_bytes=VMEM),
        cost_estimate=BRIEF,
    )(*tokens, *operands)


def pick(field, tokens):
    def plan(field_ref, mine_ref, up_ref, down_ref, theirs_ref):
        member = lax.axis_index("tm")
        moves = []
        for place in range(ROLES):
            own = field_ref.at[:, element_at(member, place, OWN)]
            moves.append((field_ref.at[:, element_at(member, place, OTHER)], theirs_ref.at[place]))
            if place > 0:
                moves.append((own, up_ref.at[place - 1]))
            if place < ROLES - 1:
                moves.append((own, down_ref.at[place]))
            moves.append((own, mine_ref.at[place]))
        return moves

    return move(plan, [field], [(count, *PIECE) for count in (ROLES, ROLES - 1, ROLES - 1, ROLES)], tokens)


def rims(field, token):
    edge = P1 * P1

    def plan(field_ref, last_ref, first_ref):
        moves = []
        for variable in range(VARS):
            target = pl.ds(variable * edge, edge)
            for ref, node in ((last_ref, P1 - 1), (first_ref, 0)):
                origin = pl.ds((variable * P1 + node) * edge, edge)
                moves.append((field_ref.at[:, :, origin], ref.at[:, :, target]))
        return moves

    return move(plan, [field], [(2, field.shape[1], FACE, RHS)] * 2, [token])


def messages(parts, tokens=()):
    def plan(*refs):
        return [
            (ref.at[first:last], target)
            for ref, target, (_, first, last) in zip(refs, refs[len(parts):], parts)
        ]

    shapes = [(last - first, *PIECE) for _, first, last in parts]
    return move(plan, [held for held, _, _ in parts], shapes, tokens)


def combine(weights, groups, dtypes, tokens=(), known=(), rows=16):
    operands, operand_of = [], {}
    for sources, _ in groups:
        for array, _, _, _ in sources:
            if id(array) not in operand_of:
                operand_of[id(array)] = len(operands)
                operands.append(array)
    for array, _ in known:
        if id(array) not in operand_of:
            operand_of[id(array)] = len(operands)
            operands.append(array)
    slots = [0] * len(dtypes)
    stores, begins = [], []
    for _, targets in groups:
        placed = []
        for step, column, output in targets:
            placed.append((step, column, output, slots[output]))
            slots[output] += 1
        stores.append(placed)
        begins.append([known[len(sum(begins, [])) + i] for i in range(len(targets))] if known else [])

    def kernel(weights_ref, *refs):
        refs = refs[len(tokens):]
        inputs, outputs = refs[: len(operands)], refs[len(operands):]
        for (sources, _), targets, begin in zip(groups, stores, begins):
            @pl.loop(0, BLOCK // rows)
            def _(chunk):
                span = pl.ds(pl.multiple_of(chunk * rows, rows), rows)
                sums = [None] * len(targets)
                for array, place, source_step, source_column in sources:
                    ref = inputs[operand_of[id(array)]]
                    first = ref[place, 0, span].astype(jnp.float32)
                    second = ref[place, 1, span].astype(jnp.float32)
                    plus, minus = first + second, first - second
                    for index, (step, column, _, _) in enumerate(targets):
                        if source_step == step and source_column == column:
                            continue
                        slot = weight_slot(source_step, step, source_column, column)
                        row, lane = divmod(slot, RHS)
                        term = (weights_ref[row, lane] * plus, weights_ref[row, lane + 1] * minus)
                        if sums[index] is None:
                            sums[index] = term
                        else:
                            sums[index] = (sums[index][0] + term[0], sums[index][1] + term[1])
                for index, ((plus, minus), (_, _, output, slot)) in enumerate(zip(sums, targets)):
                    totals = [plus + minus, plus - minus]
                    if begin:
                        array, place = begin[index]
                        ref = inputs[operand_of[id(array)]]
                        totals = [ref[place, half, span] + totals[half] for half in range(2)]
                    for half in range(2):
                        outputs[output][slot, half, span] = totals[half].astype(outputs[output].dtype)

    vmem = pl.BlockSpec(memory_space=pltpu.VMEM)
    return pl.pallas_call(
        kernel,
        in_specs=[pl.BlockSpec(memory_space=pltpu.SMEM)]
        + [pl.BlockSpec(memory_space=pl.ANY)] * len(tokens)
        + [vmem] * len(operands),
        out_specs=[vmem] * len(slots),
        out_shape=[
            jax.ShapeDtypeStruct((count, *PIECE), dtype) for count, dtype in zip(slots, dtypes)
        ],
        compiler_params=pltpu.CompilerParams(vmem_limit_bytes=VMEM),
        cost_estimate=BRIEF,
    )(weights, *tokens, *operands)


def settle(inner, first, second, tokens):
    def kernel(*refs):
        inner_ref, first_ref, second_ref, out_ref = refs[len(tokens):]
        for position, ref in enumerate((first_ref, second_ref)):
            total = inner_ref[position] + ref[1].astype(jnp.float32)
            out_ref[position] = total.astype(jnp.bfloat16)

    vmem = pl.BlockSpec(memory_space=pltpu.VMEM)
    return pl.pallas_call(
        kernel,
        in_specs=[pl.BlockSpec(memory_space=pl.ANY)] * len(tokens) + [vmem] * 3,
        out_specs=vmem,
        out_shape=jax.ShapeDtypeStruct(inner.shape, jnp.bfloat16),
        compiler_params=pltpu.CompilerParams(vmem_limit_bytes=VMEM),
        cost_estimate=BRIEF,
    )(*tokens, inner, first, second)


def finish(member, base, scale, block_inverse, places, terms, before=None):
    count = len(places)

    def element(step, member_ref):
        index = element_at(member_ref[0], *places[0])
        for position in range(1, count):
            index = jnp.where(step == position, element_at(member_ref[0], *places[position]), index)
        return index

    arrays = []
    for array, _ in sum(terms, []):
        if not any(array is known for known in arrays):
            arrays.append(array)

    def find(refs, entry):
        for ref, array in zip(refs, arrays):
            if array is entry[0]:
                return ref[entry[1]].astype(jnp.float32)

    def kernel(member_ref, base_ref, scale_ref, inverse_ref, *refs):
        out_ref, spectral = refs[-2:]
        step = pl.program_id(0)
        for position in range(count):
            @pl.when(step == position)
            def _():
                total = sum(find(refs, term) for term in terms[position])
                spectral[...] = total.astype(jnp.bfloat16)

        for half in range(2):
            mixed = spectral[half].astype(jnp.float32)
            residual = (base_ref[half, 0] - scale_ref[0] * mixed).astype(jnp.bfloat16)
            out_ref[half, 0] = jnp.dot(
                inverse_ref[half, 0], residual, preferred_element_type=jnp.float32
            ).astype(jnp.bfloat16)

    whole = pl.BlockSpec(memory_space=pltpu.VMEM)
    by_element = pl.BlockSpec((2, 1, BLOCK, RHS), lambda i, m: (0, element(i, m), 0, 0))
    operands = [base, scale, block_inverse, *arrays]
    specs = [
        by_element,
        pl.BlockSpec((1, BLOCK, RHS), lambda i, m: (element(i, m), 0, 0)),
        pl.BlockSpec((2, 1, BLOCK, BLOCK), lambda i, m: (0, element(i, m), 0, 0)),
    ] + [whole] * len(arrays)
    aliases = {}
    if before is not None:
        operands.append(before)
        specs.append(pl.BlockSpec(memory_space=pl.ANY))
        aliases = {len(operands): 0}
    return pl.pallas_call(
        kernel,
        grid_spec=pltpu.PrefetchScalarGridSpec(
            num_scalar_prefetch=1,
            grid=(count,),
            in_specs=specs,
            out_specs=by_element,
            scratch_shapes=[pltpu.VMEM(PIECE, jnp.bfloat16)],
        ),
        out_shape=jax.ShapeDtypeStruct((2, 2 * ROLES, BLOCK, RHS), jnp.bfloat16),
        input_output_aliases=aliases,
        compiler_params=pltpu.CompilerParams(vmem_limit_bytes=VMEM),
        cost_estimate=BRIEF,
    )(member, *operands)


def from_behind(value, axis, steps):
    count = lax.axis_size(axis)
    first, last = (max(0, -steps), min(count, count - steps))
    return lax.ppermute(value, axis, [(source, source + steps) for source in range(first, last)])


def trace_rows():
    rows = np.zeros((4, FACE, BLOCK), np.float32)
    for outer in range(VARS * P1):
        for inner in range(P1):
            rows[0, outer * P1 + inner, (outer * P1 + P1 - 1) * P1 + inner] = 1
            rows[1, outer * P1 + inner, outer * P1 * P1 + inner] = 1
            rows[2, outer * P1 + inner, (outer * P1 + inner) * P1 + P1 - 1] = 1
            rows[3, outer * P1 + inner, (outer * P1 + inner) * P1] = 1
    return rows.reshape(4 * FACE, BLOCK)


def transposed_dot(left, right):
    return lax.dot_general(left, right, (((0,), (0,)), ((), ())), preferred_element_type=jnp.float32)


def couple(field, lower, upper, source, face_partials, mass, tokens):
    elements = field.shape[1]

    def kernel(*refs):
        (rows_ref, field_ref, lower_ref, upper_ref, source_ref, partials_ref, mass_ref,
         out_ref, scale_ref, token_ref, picked) = refs[len(tokens):]
        element = pl.program_id(0)

        @pl.when(element == 0)
        def _():
            @pl.loop(0, elements)
            def _(index):
                for half in range(2):
                    picked[half, index] = jnp.dot(
                        rows_ref[...], field_ref[half, index], preferred_element_type=jnp.float32
                    ).astype(jnp.bfloat16)

        token_ref[...] = jnp.zeros_like(token_ref)
        row = OMEGA_TIME * mass_ref[pl.ds(element, 1), :]
        scale_ref[0] = jnp.broadcast_to(row, (RHS, BLOCK)).T
        pitch, span = element // EZ, element % EZ
        behind = (pitch + EY - 1) % EY * EZ + span
        ahead = (pitch + 1) % EY * EZ + span
        across = element + 1 - 2 * span
        for half in range(2):
            low = picked[half, across, 2 * FACE: 3 * FACE]
            high = picked[half, across, 3 * FACE: 4 * FACE]
            traces = jnp.concatenate([
                lower_ref[half, 0],
                upper_ref[half, 0],
                picked[half, behind, 0: FACE],
                picked[half, ahead, FACE: 2 * FACE],
                jnp.where(span == 1, low, jnp.zeros_like(low)),
                jnp.where(span == 0, high, jnp.zeros_like(high)),
            ])
            partials = jnp.concatenate([partials_ref[half, 0, face] for face in range(6)])
            out_ref[half, 0] = source_ref[half, 0].astype(jnp.float32) - lax.dot_general(
                partials, traces, (((0,), (0,)), ((), ())), preferred_element_type=jnp.float32
            )

    whole = pl.BlockSpec(memory_space=pltpu.VMEM)
    by_element = pl.BlockSpec((2, 1, BLOCK, RHS), lambda i: (0, i, 0, 0))
    rim = pl.BlockSpec((2, 1, FACE, RHS), lambda i: (0, i, 0, 0))
    return pl.pallas_call(
        kernel,
        grid=(elements,),
        in_specs=[pl.BlockSpec(memory_space=pl.ANY)] * len(tokens) + [
            whole, whole, rim, rim, by_element,
            pl.BlockSpec((2, 1, 6, FACE, BLOCK), lambda i: (0, i, 0, 0, 0)),
            whole,
        ],
        out_specs=[
            by_element,
            pl.BlockSpec((1, BLOCK, RHS), lambda i: (i, 0, 0)),
            pl.BlockSpec((8, RHS), lambda i: (0, 0)),
        ],
        out_shape=[
            jax.ShapeDtypeStruct(field.shape, jnp.float32),
            jax.ShapeDtypeStruct(field.shape[1:], jnp.float32),
            jax.ShapeDtypeStruct((8, RHS), jnp.float32),
        ],
        scratch_shapes=[pltpu.VMEM(field.shape, jnp.bfloat16)],
        compiler_params=pltpu.CompilerParams(vmem_limit_bytes=VMEM),
        cost_estimate=BRIEF,
    )(
        *tokens, jnp.asarray(trace_rows(), jnp.bfloat16), field, lower, upper, source,
        face_partials, mass,
    )


def per_device(adjoint, source, block_inverse, face_partials, mass):
    member = lax.axis_index("tm").reshape(1)
    field = adjoint[:, 0]
    block_inverse = block_inverse[:, 0]
    weights = move(
        lambda origin, target: [(origin.at[lax.axis_index("tm")], target)],
        [jnp.asarray(weight_table())], [(8, RHS)], dtype=jnp.float32,
    )[0]

    mine, for_up, for_down, theirs = pick(field, [member])
    other = send(theirs, 0, 1)
    up_one, down_one = [send(for_up, 1)], [send(for_down, -1)]
    last, first = rims(field, mine)
    lower_rim, upper_rim = from_behind(last, "mesh", 1), from_behind(first, "mesh", -1)
    for_up, for_down = messages([(up_one[OWN], 1, 3), (down_one[OWN], 0, 2)])
    up_two, down_two = [send(for_up, 1)], [send(for_down, -1)]
    for_up, for_down = messages(
        [(other, 1, 4), (other, 0, 3)], [for_up, lower_rim, upper_rim]
    )
    base, scale, coupled = couple(
        field, lower_rim, upper_rim, source[:, 0], face_partials[:, 0], mass, [for_up]
    )
    up_one.append(send(for_up, 1))
    down_one.append(send(for_down, -1))
    for_up, for_down = messages([(up_two[OWN], 1, 2), (down_two[OWN], 0, 1)])
    up_three, down_three = [send(for_up, 1)], [send(for_down, -1)]
    for_up, for_down = messages(
        [(up_one[OTHER], 1, 3), (down_one[OTHER], 0, 2)], [coupled]
    )
    up_two.append(send(for_up, 1))
    down_two.append(send(for_down, -1))
    for_up, for_down = messages([(up_two[OTHER], 1, 2), (down_two[OTHER], 0, 1)])
    up_three.append(send(for_up, 1))
    down_three.append(send(for_down, -1))
    up = list(zip((mine, other), up_one, up_two, up_three))
    down = list(zip((mine, other), down_one, down_two, down_three))

    def sources(entries):
        return [
            (stream[column][level], place, step, column)
            for column in (OWN, OTHER)
            for stream, level, place, step in entries
        ]

    role_one = sources([(up, 0, 0, 0), (up, 1, 0, -1), (up, 2, 0, -2), (up, 3, 0, -3)])
    role_two = sources([(down, 0, 3, 0), (down, 1, 2, 1), (down, 2, 1, 2), (down, 3, 0, 3)])
    role_zero = sources([(up, 0, 1, 0), (up, 1, 1, -1), (up, 2, 1, -2), (down, 1, 0, 1)])
    role_three = sources([(up, 0, 2, 0), (down, 1, 1, 1), (down, 2, 0, 2), (up, 1, 2, -1)])
    bf16 = jnp.bfloat16
    f32 = jnp.float32
    here = [(0, OWN, 0), (0, OTHER, 1)]

    outer_own, outer_other = combine(weights, [(role_zero, here), (role_three, here)], [f32, bf16])
    passed_outer = send(outer_other, 0, 1)
    near_up, near_down = [(1, OWN, 0), (1, OTHER, 0)], [(-1, OWN, 1), (-1, OTHER, 1)]
    begun_up, begun_down = combine(
        weights, [(role_one[:-1], near_up), (role_two[:-1], near_down)], [f32] * 2, [outer_other]
    )
    for_up, for_down = combine(
        weights,
        [(role_one[-1:], near_up), (role_two[-1:], near_down)],
        [bf16] * 2,
        known=[(begun_up, 0), (begun_up, 1), (begun_down, 0), (begun_down, 1)],
    )
    up_near, down_near = send(for_up, 1), send(for_down, -1)
    inner = [(0, OWN, 4), (0, OTHER, 5)]
    up_far, up_far_across, down_far, down_far_across, inner_own, inner_other = combine(
        weights,
        [
            (role_one, [(2, OWN, 0), (2, OTHER, 1)] + inner),
            (role_two, [(-2, OWN, 2), (-2, OTHER, 3)] + inner),
        ],
        [bf16] * 4 + [f32] * 2,
        [for_up, passed_outer],
    )
    token = up_far
    up_far, up_far_across = send(up_far, 2), send(up_far_across, 2, 1)
    down_far, down_far_across = send(down_far, -2), send(down_far_across, -2, 1)
    passed_inner = send(settle(inner_other, down_near, up_near, [token]), 0, 1)

    updated = None
    for places, terms in (
        (
            [(0, OWN), (3, OWN)],
            [[(inner_own, 0), (down_near, 0)], [(inner_own, 1), (up_near, 0)]],
        ),
        ([(0, OTHER), (3, OTHER)], [[(passed_inner, 0)], [(passed_inner, 1)]]),
        (
            [(1, OWN), (2, OWN), (1, OTHER), (2, OTHER)],
            [
                [(outer_own, 0), (down_far, 0)], [(outer_own, 1), (up_far, 0)],
                [(passed_outer, 0), (down_far_across, 0)], [(passed_outer, 1), (up_far_across, 0)],
            ],
        ),
    ):
        updated = finish(member, base, scale, block_inverse, places, terms, updated)
    return updated[:, None]


def solution(mesh):
    return jax.shard_map(
        per_device,
        mesh=mesh,
        in_specs=(
            P(None, "tm", "mesh", None, None),
            P(None, "tm", "mesh", None, None),
            P(None, "tm", "mesh", None, None),
            P(None, "tm", "mesh", None, None, None),
            P("mesh", None),
        ),
        out_specs=P(None, "tm", "mesh", None, None),
        check_vma=False,
    )
```

```python
import math

import jax
import jax.numpy as jnp
import numpy as np
from jax import lax
from jax.experimental import pallas as pl
from jax.experimental.pallas import tpu as pltpu
from jax.sharding import PartitionSpec as P

VARS = 5
P1 = 4
EY = 4
EZ = 2
RHS = 128
BLOCK = 320
FACE = 80
OMEGA_TIME = 0.25

RING = 8
TIMES = 32
HALF = 16
ROLES = 4
ORDER = (1, 0, 3, 2)
OWN, OTHER = 0, 1
FAR = 3
AHEAD = 2
PIECE = (2, BLOCK, RHS)
VMEM = 8 << 20
BRIEF = pl.CostEstimate(flops=1, bytes_accessed=1, transcendentals=0)


def spectral_weight(offset):
    offset = offset % TIMES
    if offset in (0, HALF):
        return 0.0
    return 0.5 * (-1) ** offset / math.tan(math.pi * offset / TIMES)


def weight_slot(source_step, target_step, source_column, target_column):
    row = (target_step + AHEAD) * (2 * FAR + 1) + source_step + FAR
    return 2 * (4 * row + 2 * source_column + target_column)


def weight_table():
    table = np.zeros((HALF, 8 * RHS), np.float32)
    for member in range(HALF):
        z, y = divmod(member, 2)
        for target_step in range(-AHEAD, AHEAD + 1):
            for source_step in range(-FAR, FAR + 1):
                for source_column in (OWN, OTHER):
                    for target_column in (OWN, OTHER):
                        source = (z + source_step) % RING * 2 + (y ^ source_column)
                        target = (z + target_step) % RING * 2 + (y ^ target_column)
                        near = spectral_weight(source - target)
                        far = spectral_weight(source - target + HALF)
                        slot = weight_slot(source_step, target_step, source_column, target_column)
                        table[member, slot] = 0.5 * (near + far)
                        table[member, slot + 1] = 0.5 * (near - far)
    return table.reshape(HALF, 8, RHS)


def element_at(member, place, column):
    z, y = member // 2, member % 2
    half = y if column == OWN else 1 - y
    return half * ROLES + (z + ROLES - (place ^ 1)) % ROLES


def column_pairs(step, swap):
    return [
        (z * 2 + y, (z + step) % RING * 2 + (y ^ swap)) for z in range(RING) for y in range(2)
    ]


def send(value, step, swap=0):
    return lax.ppermute(value, "tm", column_pairs(step, swap))


def move(plan, operands, shapes, tokens=(), dtype=jnp.bfloat16):
    def kernel(*refs):
        refs = refs[len(tokens):]
        copies = [
            pltpu.make_async_copy(origin, target, refs[-1].at[index])
            for index, (origin, target) in enumerate(plan(*refs[:-1]))
        ]
        for copy in copies:
            copy.start()
        for copy in copies:
            copy.wait()

    return pl.pallas_call(
        kernel,
        in_specs=[pl.BlockSpec(memory_space=pl.ANY)] * len(tokens)
        + [pl.BlockSpec(memory_space=pl.ANY)] * len(operands),
        out_specs=[pl.BlockSpec(memory_space=pl.ANY)] * len(shapes),
        out_shape=[jax.ShapeDtypeStruct(shape, dtype) for shape in shapes],
        scratch_shapes=[pltpu.SemaphoreType.DMA((32,))],
        compiler_params=pltpu.CompilerParams(vmem_limit_bytes=VMEM),
        cost_estimate=BRIEF,
    )(*tokens, *operands)


def pick(field, tokens):
    def plan(field_ref, mine_ref, up_ref, down_ref, theirs_ref):
        member = lax.axis_index("tm")
        moves = []
        for place in range(ROLES):
            own = field_ref.at[:, element_at(member, place, OWN)]
            moves.append((field_ref.at[:, element_at(member, place, OTHER)], theirs_ref.at[place]))
            if place > 0:
                moves.append((own, up_ref.at[place - 1]))
            if place < ROLES - 1:
                moves.append((own, down_ref.at[place]))
            moves.append((own, mine_ref.at[place]))
        return moves

    return move(plan, [field], [(count, *PIECE) for count in (ROLES, ROLES - 1, ROLES - 1, ROLES)], tokens)


def rims(field, token):
    edge = P1 * P1

    def plan(field_ref, last_ref, first_ref):
        moves = []
        for variable in range(VARS):
            target = pl.ds(variable * edge, edge)
            for ref, node in ((last_ref, P1 - 1), (first_ref, 0)):
                origin = pl.ds((variable * P1 + node) * edge, edge)
                moves.append((field_ref.at[:, :, origin], ref.at[:, :, target]))
        return moves

    return move(plan, [field], [(2, field.shape[1], FACE, RHS)] * 2, [token])


def messages(parts, tokens=()):
    def plan(*refs):
        return [
            (ref.at[first:last], target)
            for ref, target, (_, first, last) in zip(refs, refs[len(parts):], parts)
        ]

    shapes = [(last - first, *PIECE) for _, first, last in parts]
    return move(plan, [held for held, _, _ in parts], shapes, tokens)


def combine(weights, groups, dtypes, tokens=(), known=(), rows=16):
    operands, operand_of = [], {}
    for sources, _ in groups:
        for array, _, _, _ in sources:
            if id(array) not in operand_of:
                operand_of[id(array)] = len(operands)
                operands.append(array)
    for array, _ in known:
        if id(array) not in operand_of:
            operand_of[id(array)] = len(operands)
            operands.append(array)
    slots = [0] * len(dtypes)
    stores, begins = [], []
    for _, targets in groups:
        placed = []
        for step, column, output in targets:
            placed.append((step, column, output, slots[output]))
            slots[output] += 1
        stores.append(placed)
        begins.append([known[len(sum(begins, [])) + i] for i in range(len(targets))] if known else [])

    def kernel(weights_ref, *refs):
        refs = refs[len(tokens):]
        inputs, outputs = refs[: len(operands)], refs[len(operands):]
        for (sources, _), targets, begin in zip(groups, stores, begins):
            @pl.loop(0, BLOCK // rows)
            def _(chunk):
                span = pl.ds(pl.multiple_of(chunk * rows, rows), rows)
                sums = [None] * len(targets)
                for array, place, source_step, source_column in sources:
                    ref = inputs[operand_of[id(array)]]
                    first = ref[place, 0, span].astype(jnp.float32)
                    second = ref[place, 1, span].astype(jnp.float32)
                    plus, minus = first + second, first - second
                    for index, (step, column, _, _) in enumerate(targets):
                        if source_step == step and source_column == column:
                            continue
                        slot = weight_slot(source_step, step, source_column, column)
                        row, lane = divmod(slot, RHS)
                        term = (weights_ref[row, lane] * plus, weights_ref[row, lane + 1] * minus)
                        if sums[index] is None:
                            sums[index] = term
                        else:
                            sums[index] = (sums[index][0] + term[0], sums[index][1] + term[1])
                for index, ((plus, minus), (_, _, output, slot)) in enumerate(zip(sums, targets)):
                    totals = [plus + minus, plus - minus]
                    if begin:
                        array, place = begin[index]
                        ref = inputs[operand_of[id(array)]]
                        totals = [ref[place, half, span] + totals[half] for half in range(2)]
                    for half in range(2):
                        outputs[output][slot, half, span] = totals[half].astype(outputs[output].dtype)

    vmem = pl.BlockSpec(memory_space=pltpu.VMEM)
    return pl.pallas_call(
        kernel,
        in_specs=[pl.BlockSpec(memory_space=pltpu.SMEM)]
        + [pl.BlockSpec(memory_space=pl.ANY)] * len(tokens)
        + [vmem] * len(operands),
        out_specs=[vmem] * len(slots),
        out_shape=[
            jax.ShapeDtypeStruct((count, *PIECE), dtype) for count, dtype in zip(slots, dtypes)
        ],
        compiler_params=pltpu.CompilerParams(vmem_limit_bytes=VMEM),
        cost_estimate=BRIEF,
    )(weights, *tokens, *operands)


def settle(inner, first, second, tokens):
    def kernel(*refs):
        inner_ref, first_ref, second_ref, out_ref = refs[len(tokens):]
        for position, ref in enumerate((first_ref, second_ref)):
            total = inner_ref[position] + ref[1].astype(jnp.float32)
            out_ref[position] = total.astype(jnp.bfloat16)

    vmem = pl.BlockSpec(memory_space=pltpu.VMEM)
    return pl.pallas_call(
        kernel,
        in_specs=[pl.BlockSpec(memory_space=pl.ANY)] * len(tokens) + [vmem] * 3,
        out_specs=vmem,
        out_shape=jax.ShapeDtypeStruct(inner.shape, jnp.bfloat16),
        compiler_params=pltpu.CompilerParams(vmem_limit_bytes=VMEM),
        cost_estimate=BRIEF,
    )(*tokens, inner, first, second)


def finish(member, base, scale, block_inverse, places, terms, before=None):
    count = len(places)

    def element(step, member_ref):
        index = element_at(member_ref[0], *places[0])
        for position in range(1, count):
            index = jnp.where(step == position, element_at(member_ref[0], *places[position]), index)
        return index

    arrays = []
    for array, _ in sum(terms, []):
        if not any(array is known for known in arrays):
            arrays.append(array)

    def find(refs, entry):
        for ref, array in zip(refs, arrays):
            if array is entry[0]:
                return ref[entry[1]].astype(jnp.float32)

    def kernel(member_ref, base_ref, scale_ref, inverse_ref, *refs):
        out_ref, spectral = refs[-2:]
        step = pl.program_id(0)
        for position in range(count):
            @pl.when(step == position)
            def _():
                total = sum(find(refs, term) for term in terms[position])
                spectral[...] = total.astype(jnp.bfloat16)

        for half in range(2):
            mixed = spectral[half].astype(jnp.float32)
            residual = (base_ref[half, 0] - scale_ref[0] * mixed).astype(jnp.bfloat16)
            out_ref[half, 0] = jnp.dot(
                inverse_ref[half, 0], residual, preferred_element_type=jnp.float32
            ).astype(jnp.bfloat16)

    whole = pl.BlockSpec(memory_space=pltpu.VMEM)
    by_element = pl.BlockSpec((2, 1, BLOCK, RHS), lambda i, m: (0, element(i, m), 0, 0))
    operands = [base, scale, block_inverse, *arrays]
    specs = [
        by_element,
        pl.BlockSpec((1, BLOCK, RHS), lambda i, m: (element(i, m), 0, 0)),
        pl.BlockSpec((2, 1, BLOCK, BLOCK), lambda i, m: (0, element(i, m), 0, 0)),
    ] + [whole] * len(arrays)
    aliases = {}
    if before is not None:
        operands.append(before)
        specs.append(pl.BlockSpec(memory_space=pl.ANY))
        aliases = {len(operands): 0}
    return pl.pallas_call(
        kernel,
        grid_spec=pltpu.PrefetchScalarGridSpec(
            num_scalar_prefetch=1,
            grid=(count,),
            in_specs=specs,
            out_specs=by_element,
            scratch_shapes=[pltpu.VMEM(PIECE, jnp.bfloat16)],
        ),
        out_shape=jax.ShapeDtypeStruct((2, 2 * ROLES, BLOCK, RHS), jnp.bfloat16),
        input_output_aliases=aliases,
        compiler_params=pltpu.CompilerParams(vmem_limit_bytes=VMEM),
        cost_estimate=BRIEF,
    )(member, *operands)


def from_behind(value, axis, steps):
    count = lax.axis_size(axis)
    first, last = (max(0, -steps), min(count, count - steps))
    return lax.ppermute(value, axis, [(source, source + steps) for source in range(first, last)])


def trace_rows():
    rows = np.zeros((4, FACE, BLOCK), np.float32)
    for outer in range(VARS * P1):
        for inner in range(P1):
            rows[0, outer * P1 + inner, (outer * P1 + P1 - 1) * P1 + inner] = 1
            rows[1, outer * P1 + inner, outer * P1 * P1 + inner] = 1
            rows[2, outer * P1 + inner, (outer * P1 + inner) * P1 + P1 - 1] = 1
            rows[3, outer * P1 + inner, (outer * P1 + inner) * P1] = 1
    return rows.reshape(4 * FACE, BLOCK)


def transposed_dot(left, right):
    return lax.dot_general(left, right, (((0,), (0,)), ((), ())), preferred_element_type=jnp.float32)


def couple(field, lower, upper, source, face_partials, mass, tokens):
    elements = field.shape[1]

    def kernel(*refs):
        (rows_ref, field_ref, lower_ref, upper_ref, source_ref, partials_ref, mass_ref,
         out_ref, scale_ref, token_ref, picked) = refs[len(tokens):]
        element = pl.program_id(0)

        @pl.when(element == 0)
        def _():
            @pl.loop(0, elements)
            def _(index):
                for half in range(2):
                    picked[half, index] = jnp.dot(
                        rows_ref[...], field_ref[half, index], preferred_element_type=jnp.float32
                    ).astype(jnp.bfloat16)

        token_ref[...] = jnp.zeros_like(token_ref)
        row = OMEGA_TIME * mass_ref[pl.ds(element, 1), :]
        scale_ref[0] = jnp.broadcast_to(row, (RHS, BLOCK)).T
        pitch, span = element // EZ, element % EZ
        behind = (pitch + EY - 1) % EY * EZ + span
        ahead = (pitch + 1) % EY * EZ + span
        across = element + 1 - 2 * span
        for half in range(2):
            low = picked[half, across, 2 * FACE: 3 * FACE]
            high = picked[half, across, 3 * FACE: 4 * FACE]
            traces = jnp.concatenate([
                lower_ref[half, 0],
                upper_ref[half, 0],
                picked[half, behind, 0: FACE],
                picked[half, ahead, FACE: 2 * FACE],
                jnp.where(span == 1, low, jnp.zeros_like(low)),
                jnp.where(span == 0, high, jnp.zeros_like(high)),
            ])
            partials = jnp.concatenate([partials_ref[half, 0, face] for face in range(6)])
            out_ref[half, 0] = source_ref[half, 0].astype(jnp.float32) - lax.dot_general(
                partials, traces, (((0,), (0,)), ((), ())), preferred_element_type=jnp.float32
            )

    whole = pl.BlockSpec(memory_space=pltpu.VMEM)
    by_element = pl.BlockSpec((2, 1, BLOCK, RHS), lambda i: (0, i, 0, 0))
    rim = pl.BlockSpec((2, 1, FACE, RHS), lambda i: (0, i, 0, 0))
    return pl.pallas_call(
        kernel,
        grid=(elements,),
        in_specs=[pl.BlockSpec(memory_space=pl.ANY)] * len(tokens) + [
            whole, whole, rim, rim, by_element,
            pl.BlockSpec((2, 1, 6, FACE, BLOCK), lambda i: (0, i, 0, 0, 0)),
            whole,
        ],
        out_specs=[
            by_element,
            pl.BlockSpec((1, BLOCK, RHS), lambda i: (i, 0, 0)),
            pl.BlockSpec((8, RHS), lambda i: (0, 0)),
        ],
        out_shape=[
            jax.ShapeDtypeStruct(field.shape, jnp.float32),
            jax.ShapeDtypeStruct(field.shape[1:], jnp.float32),
            jax.ShapeDtypeStruct((8, RHS), jnp.float32),
        ],
        scratch_shapes=[pltpu.VMEM(field.shape, jnp.bfloat16)],
        compiler_params=pltpu.CompilerParams(vmem_limit_bytes=VMEM),
        cost_estimate=BRIEF,
    )(
        *tokens, jnp.asarray(trace_rows(), jnp.bfloat16), field, lower, upper, source,
        face_partials, mass,
    )


def per_device(adjoint, source, block_inverse, face_partials, mass):
    member = lax.axis_index("tm").reshape(1)
    field = adjoint[:, 0]
    block_inverse = block_inverse[:, 0]
    weights = move(
        lambda origin, target: [(origin.at[lax.axis_index("tm")], target)],
        [jnp.asarray(weight_table())], [(8, RHS)], dtype=jnp.float32,
    )[0]

    mine, for_up, for_down, theirs = pick(field, [member])
    other = send(theirs, 0, 1)
    up_one, down_one = [send(for_up, 1)], [send(for_down, -1)]
    last, first = rims(field, mine)
    lower_rim, upper_rim = from_behind(last, "mesh", 1), from_behind(first, "mesh", -1)
    for_up, = messages([(up_one[OWN], 1, 3)])
    for_down, = messages([(down_one[OWN], 0, 2)])
    up_two, down_two = [send(for_up, 1)], [send(for_down, -1)]
    for_up, for_down = messages(
        [(other, 1, 4), (other, 0, 3)], [for_up, lower_rim, upper_rim]
    )
    base, scale, coupled = couple(
        field, lower_rim, upper_rim, source[:, 0], face_partials[:, 0], mass, [for_up]
    )
    up_one.append(send(for_up, 1))
    down_one.append(send(for_down, -1))
    for_up, for_down = messages([(up_two[OWN], 1, 2), (down_two[OWN], 0, 1)])
    up_three, down_three = [send(for_up, 1)], [send(for_down, -1)]
    for_up, for_down = messages(
        [(up_one[OTHER], 1, 3), (down_one[OTHER], 0, 2)], [coupled]
    )
    up_two.append(send(for_up, 1))
    down_two.append(send(for_down, -1))
    for_up, for_down = messages([(up_two[OTHER], 1, 2), (down_two[OTHER], 0, 1)])
    up_three.append(send(for_up, 1))
    down_three.append(send(for_down, -1))
    up = list(zip((mine, other), up_one, up_two, up_three))
    down = list(zip((mine, other), down_one, down_two, down_three))

    def sources(entries):
        return [
            (stream[column][level], place, step, column)
            for column in (OWN, OTHER)
            for stream, level, place, step in entries
        ]

    role_one = sources([(up, 0, 0, 0), (up, 1, 0, -1), (up, 2, 0, -2), (up, 3, 0, -3)])
    role_two = sources([(down, 0, 3, 0), (down, 1, 2, 1), (down, 2, 1, 2), (down, 3, 0, 3)])
    role_zero = sources([(up, 0, 1, 0), (up, 1, 1, -1), (up, 2, 1, -2), (down, 1, 0, 1)])
    role_three = sources([(up, 0, 2, 0), (down, 1, 1, 1), (down, 2, 0, 2), (up, 1, 2, -1)])
    bf16 = jnp.bfloat16
    f32 = jnp.float32
    here = [(0, OWN, 0), (0, OTHER, 1)]

    outer_own, outer_other = combine(weights, [(role_zero, here), (role_three, here)], [f32, bf16])
    passed_outer = send(outer_other, 0, 1)
    near_up, near_down = [(1, OWN, 0), (1, OTHER, 0)], [(-1, OWN, 1), (-1, OTHER, 1)]
    begun_up, begun_down = combine(
        weights, [(role_one[:-1], near_up), (role_two[:-1], near_down)], [f32] * 2, [outer_other]
    )
    for_up, for_down = combine(
        weights,
        [(role_one[-1:], near_up), (role_two[-1:], near_down)],
        [bf16] * 2,
        known=[(begun_up, 0), (begun_up, 1), (begun_down, 0), (begun_down, 1)],
    )
    up_near, down_near = send(for_up, 1), send(for_down, -1)
    inner = [(0, OWN, 4), (0, OTHER, 5)]
    up_far, up_far_across, down_far, down_far_across, inner_own, inner_other = combine(
        weights,
        [
            (role_one, [(2, OWN, 0), (2, OTHER, 1)] + inner),
            (role_two, [(-2, OWN, 2), (-2, OTHER, 3)] + inner),
        ],
        [bf16] * 4 + [f32] * 2,
        [for_up, passed_outer],
    )
    token = up_far
    up_far, up_far_across = send(up_far, 2), send(up_far_across, 2, 1)
    down_far, down_far_across = send(down_far, -2), send(down_far_across, -2, 1)
    passed_inner = send(settle(inner_other, down_near, up_near, [token]), 0, 1)

    updated = None
    for places, terms in (
        (
            [(0, OWN), (3, OWN)],
            [[(inner_own, 0), (down_near, 0)], [(inner_own, 1), (up_near, 0)]],
        ),
        ([(0, OTHER), (3, OTHER)], [[(passed_inner, 0)], [(passed_inner, 1)]]),
        (
            [(1, OWN), (2, OWN), (1, OTHER), (2, OTHER)],
            [
                [(outer_own, 0), (down_far, 0)], [(outer_own, 1), (up_far, 0)],
                [(passed_outer, 0), (down_far_across, 0)], [(passed_outer, 1), (up_far_across, 0)],
            ],
        ),
    ):
        updated = finish(member, base, scale, block_inverse, places, terms, updated)
    return updated[:, None]


def solution(mesh):
    return jax.shard_map(
        per_device,
        mesh=mesh,
        in_specs=(
            P(None, "tm", "mesh", None, None),
            P(None, "tm", "mesh", None, None),
            P(None, "tm", "mesh", None, None),
            P(None, "tm", "mesh", None, None, None),
            P("mesh", None),
        ),
        out_specs=P(None, "tm", "mesh", None, None),
        check_vma=False,
    )
```

```python
import math

import jax
import jax.numpy as jnp
import numpy as np
from jax import lax
from jax.experimental import pallas as pl
from jax.experimental.pallas import tpu as pltpu
from jax.sharding import PartitionSpec as P

VARS = 5
P1 = 4
EY = 4
EZ = 2
RHS = 128
BLOCK = 320
FACE = 80
OMEGA_TIME = 0.25

RING = 8
TIMES = 32
HALF = 16
ROLES = 4
ORDER = (1, 0, 3, 2)
OWN, OTHER = 0, 1
FAR = 3
AHEAD = 2
PIECE = (2, BLOCK, RHS)
VMEM = 8 << 20
BRIEF = pl.CostEstimate(flops=1, bytes_accessed=1, transcendentals=0)


def spectral_weight(offset):
    offset = offset % TIMES
    if offset in (0, HALF):
        return 0.0
    return 0.5 * (-1) ** offset / math.tan(math.pi * offset / TIMES)


def weight_slot(source_step, target_step, source_column, target_column):
    row = (target_step + AHEAD) * (2 * FAR + 1) + source_step + FAR
    return 2 * (4 * row + 2 * source_column + target_column)


def weight_table():
    table = np.zeros((HALF, 8 * RHS), np.float32)
    for member in range(HALF):
        z, y = divmod(member, 2)
        for target_step in range(-AHEAD, AHEAD + 1):
            for source_step in range(-FAR, FAR + 1):
                for source_column in (OWN, OTHER):
                    for target_column in (OWN, OTHER):
                        source = (z + source_step) % RING * 2 + (y ^ source_column)
                        target = (z + target_step) % RING * 2 + (y ^ target_column)
                        near = spectral_weight(source - target)
                        far = spectral_weight(source - target + HALF)
                        slot = weight_slot(source_step, target_step, source_column, target_column)
                        table[member, slot] = 0.5 * (near + far)
                        table[member, slot + 1] = 0.5 * (near - far)
    return table.reshape(HALF, 8, RHS)


def element_at(member, place, column):
    z, y = member // 2, member % 2
    half = y if column == OWN else 1 - y
    return half * ROLES + (z + ROLES - (place ^ 1)) % ROLES


def column_pairs(step, swap):
    return [
        (z * 2 + y, (z + step) % RING * 2 + (y ^ swap)) for z in range(RING) for y in range(2)
    ]


def send(value, step, swap=0):
    return lax.ppermute(value, "tm", column_pairs(step, swap))


def move(plan, operands, shapes, tokens=(), dtype=jnp.bfloat16):
    def kernel(*refs):
        refs = refs[len(tokens):]
        copies = [
            pltpu.make_async_copy(origin, target, refs[-1].at[index])
            for index, (origin, target) in enumerate(plan(*refs[:-1]))
        ]
        for copy in copies:
            copy.start()
        for copy in copies:
            copy.wait()

    return pl.pallas_call(
        kernel,
        in_specs=[pl.BlockSpec(memory_space=pl.ANY)] * len(tokens)
        + [pl.BlockSpec(memory_space=pl.ANY)] * len(operands),
        out_specs=[pl.BlockSpec(memory_space=pl.ANY)] * len(shapes),
        out_shape=[jax.ShapeDtypeStruct(shape, dtype) for shape in shapes],
        scratch_shapes=[pltpu.SemaphoreType.DMA((32,))],
        compiler_params=pltpu.CompilerParams(vmem_limit_bytes=VMEM),
        cost_estimate=BRIEF,
    )(*tokens, *operands)


def pick(field, tokens):
    def plan(field_ref, mine_ref, up_ref, down_ref, theirs_ref):
        member = lax.axis_index("tm")
        moves = []
        for place in range(ROLES):
            own = field_ref.at[:, element_at(member, place, OWN)]
            moves.append((field_ref.at[:, element_at(member, place, OTHER)], theirs_ref.at[place]))
            if place > 0:
                moves.append((own, up_ref.at[place - 1]))
            if place < ROLES - 1:
                moves.append((own, down_ref.at[place]))
            moves.append((own, mine_ref.at[place]))
        return moves

    return move(plan, [field], [(count, *PIECE) for count in (ROLES, ROLES - 1, ROLES - 1, ROLES)], tokens)


def rims(field, token):
    edge = P1 * P1

    def plan(field_ref, last_ref, first_ref):
        moves = []
        for variable in range(VARS):
            target = pl.ds(variable * edge, edge)
            for ref, node in ((last_ref, P1 - 1), (first_ref, 0)):
                origin = pl.ds((variable * P1 + node) * edge, edge)
                moves.append((field_ref.at[:, :, origin], ref.at[:, :, target]))
        return moves

    return move(plan, [field], [(2, field.shape[1], FACE, RHS)] * 2, [token])


def messages(parts, tokens=()):
    def plan(*refs):
        return [
            (ref.at[first:last], target)
            for ref, target, (_, first, last) in zip(refs, refs[len(parts):], parts)
        ]

    shapes = [(last - first, *PIECE) for _, first, last in parts]
    return move(plan, [held for held, _, _ in parts], shapes, tokens)


def combine(weights, groups, dtypes, tokens=(), known=(), rows=16):
    operands, operand_of = [], {}
    for sources, _ in groups:
        for array, _, _, _ in sources:
            if id(array) not in operand_of:
                operand_of[id(array)] = len(operands)
                operands.append(array)
    for array, _ in known:
        if id(array) not in operand_of:
            operand_of[id(array)] = len(operands)
            operands.append(array)
    slots = [0] * len(dtypes)
    stores, begins = [], []
    for _, targets in groups:
        placed = []
        for step, column, output in targets:
            placed.append((step, column, output, slots[output]))
            slots[output] += 1
        stores.append(placed)
        begins.append([known[len(sum(begins, [])) + i] for i in range(len(targets))] if known else [])

    def kernel(weights_ref, *refs):
        refs = refs[len(tokens):]
        inputs, outputs = refs[: len(operands)], refs[len(operands):]
        for (sources, _), targets, begin in zip(groups, stores, begins):
            @pl.loop(0, BLOCK // rows)
            def _(chunk):
                span = pl.ds(pl.multiple_of(chunk * rows, rows), rows)
                sums = [None] * len(targets)
                for array, place, source_step, source_column in sources:
                    ref = inputs[operand_of[id(array)]]
                    first = ref[place, 0, span].astype(jnp.float32)
                    second = ref[place, 1, span].astype(jnp.float32)
                    plus, minus = first + second, first - second
                    for index, (step, column, _, _) in enumerate(targets):
                        if source_step == step and source_column == column:
                            continue
                        slot = weight_slot(source_step, step, source_column, column)
                        row, lane = divmod(slot, RHS)
                        term = (weights_ref[row, lane] * plus, weights_ref[row, lane + 1] * minus)
                        if sums[index] is None:
                            sums[index] = term
                        else:
                            sums[index] = (sums[index][0] + term[0], sums[index][1] + term[1])
                for index, ((plus, minus), (_, _, output, slot)) in enumerate(zip(sums, targets)):
                    totals = [plus + minus, plus - minus]
                    if begin:
                        array, place = begin[index]
                        ref = inputs[operand_of[id(array)]]
                        totals = [ref[place, half, span] + totals[half] for half in range(2)]
                    for half in range(2):
                        outputs[output][slot, half, span] = totals[half].astype(outputs[output].dtype)

    vmem = pl.BlockSpec(memory_space=pltpu.VMEM)
    return pl.pallas_call(
        kernel,
        in_specs=[pl.BlockSpec(memory_space=pltpu.SMEM)]
        + [pl.BlockSpec(memory_space=pl.ANY)] * len(tokens)
        + [vmem] * len(operands),
        out_specs=[vmem] * len(slots),
        out_shape=[
            jax.ShapeDtypeStruct((count, *PIECE), dtype) for count, dtype in zip(slots, dtypes)
        ],
        compiler_params=pltpu.CompilerParams(vmem_limit_bytes=VMEM),
        cost_estimate=BRIEF,
    )(weights, *tokens, *operands)


def settle(inner, first, second, tokens):
    def kernel(*refs):
        inner_ref, first_ref, second_ref, out_ref = refs[len(tokens):]
        for position, ref in enumerate((first_ref, second_ref)):
            total = inner_ref[position] + ref[1].astype(jnp.float32)
            out_ref[position] = total.astype(jnp.bfloat16)

    vmem = pl.BlockSpec(memory_space=pltpu.VMEM)
    return pl.pallas_call(
        kernel,
        in_specs=[pl.BlockSpec(memory_space=pl.ANY)] * len(tokens) + [vmem] * 3,
        out_specs=vmem,
        out_shape=jax.ShapeDtypeStruct(inner.shape, jnp.bfloat16),
        compiler_params=pltpu.CompilerParams(vmem_limit_bytes=VMEM),
        cost_estimate=BRIEF,
    )(*tokens, inner, first, second)


def finish(member, base, scale, block_inverse, places, terms, before=None):
    count = len(places)

    def element(step, member_ref):
        index = element_at(member_ref[0], *places[0])
        for position in range(1, count):
            index = jnp.where(step == position, element_at(member_ref[0], *places[position]), index)
        return index

    arrays = []
    for array, _ in sum(terms, []):
        if not any(array is known for known in arrays):
            arrays.append(array)

    def find(refs, entry):
        for ref, array in zip(refs, arrays):
            if array is entry[0]:
                return ref[entry[1]].astype(jnp.float32)

    def kernel(member_ref, base_ref, scale_ref, inverse_ref, *refs):
        out_ref, spectral = refs[-2:]
        step = pl.program_id(0)
        for position in range(count):
            @pl.when(step == position)
            def _():
                total = sum(find(refs, term) for term in terms[position])
                spectral[...] = total.astype(jnp.bfloat16)

        for half in range(2):
            mixed = spectral[half].astype(jnp.float32)
            residual = (base_ref[half, 0] - scale_ref[0] * mixed).astype(jnp.bfloat16)
            out_ref[half, 0] = jnp.dot(
                inverse_ref[half, 0], residual, preferred_element_type=jnp.float32
            ).astype(jnp.bfloat16)

    whole = pl.BlockSpec(memory_space=pltpu.VMEM)
    by_element = pl.BlockSpec((2, 1, BLOCK, RHS), lambda i, m: (0, element(i, m), 0, 0))
    operands = [base, scale, block_inverse, *arrays]
    specs = [
        by_element,
        pl.BlockSpec((1, BLOCK, RHS), lambda i, m: (element(i, m), 0, 0)),
        pl.BlockSpec((2, 1, BLOCK, BLOCK), lambda i, m: (0, element(i, m), 0, 0)),
    ] + [whole] * len(arrays)
    aliases = {}
    if before is not None:
        operands.append(before)
        specs.append(pl.BlockSpec(memory_space=pl.ANY))
        aliases = {len(operands): 0}
    return pl.pallas_call(
        kernel,
        grid_spec=pltpu.PrefetchScalarGridSpec(
            num_scalar_prefetch=1,
            grid=(count,),
            in_specs=specs,
            out_specs=by_element,
            scratch_shapes=[pltpu.VMEM(PIECE, jnp.bfloat16)],
        ),
        out_shape=jax.ShapeDtypeStruct((2, 2 * ROLES, BLOCK, RHS), jnp.bfloat16),
        input_output_aliases=aliases,
        compiler_params=pltpu.CompilerParams(vmem_limit_bytes=VMEM),
        cost_estimate=BRIEF,
    )(member, *operands)


def from_behind(value, axis, steps):
    count = lax.axis_size(axis)
    first, last = (max(0, -steps), min(count, count - steps))
    return lax.ppermute(value, axis, [(source, source + steps) for source in range(first, last)])


def trace_rows():
    rows = np.zeros((4, FACE, BLOCK), np.float32)
    for outer in range(VARS * P1):
        for inner in range(P1):
            rows[0, outer * P1 + inner, (outer * P1 + P1 - 1) * P1 + inner] = 1
            rows[1, outer * P1 + inner, outer * P1 * P1 + inner] = 1
            rows[2, outer * P1 + inner, (outer * P1 + inner) * P1 + P1 - 1] = 1
            rows[3, outer * P1 + inner, (outer * P1 + inner) * P1] = 1
    return rows.reshape(4 * FACE, BLOCK)


def transposed_dot(left, right):
    return lax.dot_general(left, right, (((0,), (0,)), ((), ())), preferred_element_type=jnp.float32)


def couple(field, lower, upper, source, face_partials, mass, tokens):
    elements = field.shape[1]

    def kernel(*refs):
        (rows_ref, field_ref, lower_ref, upper_ref, source_ref, partials_ref, mass_ref,
         out_ref, scale_ref, token_ref, picked) = refs[len(tokens):]
        element = pl.program_id(0)

        @pl.when(element == 0)
        def _():
            @pl.loop(0, elements)
            def _(index):
                for half in range(2):
                    picked[half, index] = jnp.dot(
                        rows_ref[...], field_ref[half, index], preferred_element_type=jnp.float32
                    ).astype(jnp.bfloat16)

        token_ref[...] = jnp.zeros_like(token_ref)
        row = OMEGA_TIME * mass_ref[pl.ds(element, 1), :]
        scale_ref[0] = jnp.broadcast_to(row, (RHS, BLOCK)).T
        pitch, span = element // EZ, element % EZ
        behind = (pitch + EY - 1) % EY * EZ + span
        ahead = (pitch + 1) % EY * EZ + span
        across = element + 1 - 2 * span
        for half in range(2):
            low = picked[half, across, 2 * FACE: 3 * FACE]
            high = picked[half, across, 3 * FACE: 4 * FACE]
            traces = jnp.concatenate([
                lower_ref[half, 0],
                upper_ref[half, 0],
                picked[half, behind, 0: FACE],
                picked[half, ahead, FACE: 2 * FACE],
                jnp.where(span == 1, low, jnp.zeros_like(low)),
                jnp.where(span == 0, high, jnp.zeros_like(high)),
            ])
            partials = jnp.concatenate([partials_ref[half, 0, face] for face in range(6)])
            out_ref[half, 0] = source_ref[half, 0].astype(jnp.float32) - lax.dot_general(
                partials, traces, (((0,), (0,)), ((), ())), preferred_element_type=jnp.float32
            )

    whole = pl.BlockSpec(memory_space=pltpu.VMEM)
    by_element = pl.BlockSpec((2, 1, BLOCK, RHS), lambda i: (0, i, 0, 0))
    rim = pl.BlockSpec((2, 1, FACE, RHS), lambda i: (0, i, 0, 0))
    return pl.pallas_call(
        kernel,
        grid=(elements,),
        in_specs=[pl.BlockSpec(memory_space=pl.ANY)] * len(tokens) + [
            whole, whole, rim, rim, by_element,
            pl.BlockSpec((2, 1, 6, FACE, BLOCK), lambda i: (0, i, 0, 0, 0)),
            whole,
        ],
        out_specs=[
            by_element,
            pl.BlockSpec((1, BLOCK, RHS), lambda i: (i, 0, 0)),
            pl.BlockSpec((8, RHS), lambda i: (0, 0)),
        ],
        out_shape=[
            jax.ShapeDtypeStruct(field.shape, jnp.float32),
            jax.ShapeDtypeStruct(field.shape[1:], jnp.float32),
            jax.ShapeDtypeStruct((8, RHS), jnp.float32),
        ],
        scratch_shapes=[pltpu.VMEM(field.shape, jnp.bfloat16)],
        compiler_params=pltpu.CompilerParams(vmem_limit_bytes=VMEM),
        cost_estimate=BRIEF,
    )(
        *tokens, jnp.asarray(trace_rows(), jnp.bfloat16), field, lower, upper, source,
        face_partials, mass,
    )


def per_device(adjoint, source, block_inverse, face_partials, mass):
    member = lax.axis_index("tm").reshape(1)
    field = adjoint[:, 0]
    block_inverse = block_inverse[:, 0]
    weights = move(
        lambda origin, target: [(origin.at[lax.axis_index("tm")], target)],
        [jnp.asarray(weight_table())], [(8, RHS)], dtype=jnp.float32,
    )[0]

    mine, for_up, for_down, theirs = pick(field, [member])
    other = send(theirs, 0, 1)
    up_one, down_one = [send(for_up, 1)], [send(for_down, -1)]
    last, first = rims(field, mine)
    lower_rim, upper_rim = from_behind(last, "mesh", 1), from_behind(first, "mesh", -1)
    for_up, = messages([(up_one[OWN], 1, 3)])
    for_down, = messages([(down_one[OWN], 0, 2)])
    up_two, down_two = [send(for_up, 1)], [send(for_down, -1)]
    for_up, for_down = messages(
        [(other, 1, 4), (other, 0, 3)], [for_up, lower_rim, upper_rim]
    )
    base, scale, coupled = couple(
        field, lower_rim, upper_rim, source[:, 0], face_partials[:, 0], mass, [for_up]
    )
    up_one.append(send(for_up, 1))
    down_one.append(send(for_down, -1))
    for_up, for_down = messages([(up_two[OWN], 1, 2), (down_two[OWN], 0, 1)])
    up_three, down_three = [send(for_up, 1)], [send(for_down, -1)]
    for_up, = messages([(up_one[OTHER], 1, 3)], [coupled])
    for_down, = messages([(down_one[OTHER], 0, 2)], [coupled])
    up_two.append(send(for_up, 1))
    down_two.append(send(for_down, -1))
    for_up, = messages([(up_two[OTHER], 1, 2)])
    for_down, = messages([(down_two[OTHER], 0, 1)])
    up_three.append(send(for_up, 1))
    down_three.append(send(for_down, -1))
    up = list(zip((mine, other), up_one, up_two, up_three))
    down = list(zip((mine, other), down_one, down_two, down_three))

    def sources(entries):
        return [
            (stream[column][level], place, step, column)
            for column in (OWN, OTHER)
            for stream, level, place, step in entries
        ]

    role_one = sources([(up, 0, 0, 0), (up, 1, 0, -1), (up, 2, 0, -2), (up, 3, 0, -3)])
    role_two = sources([(down, 0, 3, 0), (down, 1, 2, 1), (down, 2, 1, 2), (down, 3, 0, 3)])
    role_zero = sources([(up, 0, 1, 0), (up, 1, 1, -1), (up, 2, 1, -2), (down, 1, 0, 1)])
    role_three = sources([(up, 0, 2, 0), (down, 1, 1, 1), (down, 2, 0, 2), (up, 1, 2, -1)])
    bf16 = jnp.bfloat16
    f32 = jnp.float32
    here = [(0, OWN, 0), (0, OTHER, 1)]

    outer_own, outer_other = combine(weights, [(role_zero, here), (role_three, here)], [f32, bf16])
    passed_outer = send(outer_other, 0, 1)
    near_up, near_down = [(1, OWN, 0), (1, OTHER, 0)], [(-1, OWN, 1), (-1, OTHER, 1)]
    begun_up, begun_down = combine(
        weights, [(role_one[:-1], near_up), (role_two[:-1], near_down)], [f32] * 2, [outer_other]
    )
    for_up, for_down = combine(
        weights,
        [(role_one[-1:], near_up), (role_two[-1:], near_down)],
        [bf16] * 2,
        known=[(begun_up, 0), (begun_up, 1), (begun_down, 0), (begun_down, 1)],
    )
    up_near, down_near = send(for_up, 1), send(for_down, -1)
    inner = [(0, OWN, 4), (0, OTHER, 5)]
    up_far, up_far_across, down_far, down_far_across, inner_own, inner_other = combine(
        weights,
        [
            (role_one, [(2, OWN, 0), (2, OTHER, 1)] + inner),
            (role_two, [(-2, OWN, 2), (-2, OTHER, 3)] + inner),
        ],
        [bf16] * 4 + [f32] * 2,
        [for_up, passed_outer],
    )
    token = up_far
    up_far, up_far_across = send(up_far, 2), send(up_far_across, 2, 1)
    down_far, down_far_across = send(down_far, -2), send(down_far_across, -2, 1)
    passed_inner = send(settle(inner_other, down_near, up_near, [token]), 0, 1)

    updated = None
    for places, terms in (
        (
            [(0, OWN), (3, OWN)],
            [[(inner_own, 0), (down_near, 0)], [(inner_own, 1), (up_near, 0)]],
        ),
        ([(0, OTHER), (3, OTHER)], [[(passed_inner, 0)], [(passed_inner, 1)]]),
        (
            [(1, OWN), (2, OWN), (1, OTHER), (2, OTHER)],
            [
                [(outer_own, 0), (down_far, 0)], [(outer_own, 1), (up_far, 0)],
                [(passed_outer, 0), (down_far_across, 0)], [(passed_outer, 1), (up_far_across, 0)],
            ],
        ),
    ):
        updated = finish(member, base, scale, block_inverse, places, terms, updated)
    return updated[:, None]


def solution(mesh):
    return jax.shard_map(
        per_device,
        mesh=mesh,
        in_specs=(
            P(None, "tm", "mesh", None, None),
            P(None, "tm", "mesh", None, None),
            P(None, "tm", "mesh", None, None),
            P(None, "tm", "mesh", None, None, None),
            P("mesh", None),
        ),
        out_specs=P(None, "tm", "mesh", None, None),
        check_vma=False,
    )
```
